32 devices in a mesh: slab: 4 (over x, core), tile: 8 (over z, y).
Axes of the slice: x: 2, y: 2, z: 4, core: 2. Of those that a mesh axis runs over, the one named last changes fastest.
Arguments:
- right_side: float32 [32, 128, 128], P('slab', 'tile'), may hold values from -8 to 8
- diagonal: float32 [32, 128, 128], P('slab', 'tile'), may hold values from 0.25 to 2
- inlet_index: int32 [4, 8, 32, 16], P('slab', 'tile'), may hold values from 0 to 16383
- plate_order: int32 [32], replicated, may hold values from 0 to 31, each once
- conductance: float32 [32], P('tile'), may hold values from 0.5 to 2
- plate_level: float32 [32], P('tile'), may hold values from -3 to 3
Outputs:
- solution: float32 [32, 128, 128], P('slab', 'tile')
- residual: float32 [32, 128, 128], P('slab', 'tile')
- inlet_flow: float32 [32], P('tile')
The draws below stay inside these ranges and needn't reach their ends.
Inputs may be any that keep to these rules, and one draw needn't show every extreme that they name: `inlet_index`: each entry is a cell of the block of the device given by the first two indices. `plate_order`: each plate appears once.
All inputs are finite; a program needn't handle non-finite values.
Results may differ from the reference program's by a relative error of at most 0.0003.
Values sent between devices are 32-bit elements; how exact they have to be, the bound alone decides.
A program may use at most 64 MiB of HBM per device.

```python
import math
import jax
import jax.numpy as jnp
from jax import lax

CZ = 8
CY = 16
NX = 128
STEPS = 4
BLOCKS = 2
INLETS = 16
NZ = 32
NY = 128
PLATES = 32
N_SLAB = 4
N_TILE = 8


def set_ends(array, own_key, least, largest):
    spot = [jax.random.randint(jax.random.fold_in(own_key, axis), (), 0, length) for axis, length in enumerate(array.shape)]
    main_axis = array.shape.index(max(array.shape))
    neighbour = spot[:main_axis] + [(spot[main_axis] + 1) % array.shape[main_axis]] + spot[main_axis + 1:]
    return array.at[tuple(spot)].set(least).at[tuple(neighbour)].set(largest)


def block_scale(own_key, extent, cuts, low, high):
    level, own = 1.0, jax.random.fold_in(own_key, 6)
    for dim, shards_of in cuts:
        steps = jnp.exp(jax.random.uniform(jax.random.fold_in(own, dim), (shards_of,), jnp.float32, low / len(cuts), high / len(cuts)))
        level = level * jnp.repeat(steps, extent[dim] // shards_of).reshape([-1 if axis == dim else 1 for axis in range(len(extent))])
    return level


def scatter_about(rng, shape, spread, bound, split=(), dtype=jnp.bfloat16):
    values = jax.random.normal(rng, shape, jnp.float32) * spread
    if len(split) > 0:
        values = block_scale(rng, shape, split, -0.22, 0.18) * values
    return jnp.clip(values, min=-bound, max=bound).astype(dtype)


def setup_inputs(seed: int = 0) -> dict:
    splits = jax.random.split(jax.random.key(seed), 7)
    right_side = scatter_about(splits[0], (NZ, NY, NX), 1.0, 8.0, ((0, 4), (1, 8)), jnp.float32)
    diagonal = jnp.clip(0.25 + 1.75 * jax.random.uniform(splits[1], (NZ, NY, NX), jnp.float32) ** block_scale(splits[1], (NZ, NY, NX), ((0, 4), (1, 8)), -0.2, 0.2), 0.25, 2.0)
    inlet_index = set_ends(jax.random.randint(splits[2], (N_SLAB, N_TILE, PLATES, INLETS), 0, CZ * CY * NX), jax.random.fold_in(splits[2], 1), 0, (CZ * CY * NX) - 1).astype(jnp.int32)
    plate_order = jax.random.permutation(splits[3], PLATES).astype(jnp.int32)
    conductance = jnp.clip(jnp.exp(math.log(2.0) - 1.3862944 * jax.random.uniform(splits[4], (PLATES,), jnp.float32) ** block_scale(splits[4], (PLATES,), ((0, 8),), -0.2, 0.2)), 0.5, 2.0)
    plate_level = scatter_about(splits[5], (PLATES,), 0.5, 3.0, ((0, 8),), jnp.float32)
    return {"right_side": right_side, "diagonal": diagonal, "inlet_index": inlet_index, "plate_order": plate_order, "conductance": conductance, "plate_level": plate_level}


GRAM_PAIRS = [(row_at, col_at) for row_at in range(5) for col_at in range(row_at, 5)]

def apply_shifted(padded, diagonal):
    center = padded[1:-1, 1:-1]
    zero_col = jnp.zeros_like(center[:, :, :1])
    beside = padded[2:, 1:-1] + padded[:-2, 1:-1]
    beside = beside + padded[1:-1, 2:] + padded[1:-1, :-2]
    beside = beside + jnp.concatenate([center[:, :, 1:], zero_col], axis=2) + jnp.concatenate([zero_col, center[:, :, :-1]], axis=2)
    return ((diagonal - 1.0) * center - beside) / 7.0

def cholesky_solve(matrix, rhs):
    factor = jnp.linalg.cholesky(matrix)
    forward = []
    for row_at in range(4):
        value = rhs[row_at]
        for col_at in range(row_at):
            value = value - factor[row_at, col_at] * forward[col_at]
        forward.append(value / factor[row_at, row_at])
    backward = [None] * 4
    for row_at in range(3, -1, -1):
        value = forward[row_at]
        for col_at in range(row_at + 1, 4):
            value = value - factor[col_at, row_at] * backward[col_at]
        backward[row_at] = value / factor[row_at, row_at]
    return jnp.stack(backward)

def solve_block(gram_vec):
    entries = {}
    for place, pair in enumerate(GRAM_PAIRS):
        entries[pair] = gram_vec[place]
        entries[pair[1], pair[0]] = gram_vec[place]
    gram = jnp.stack([jnp.stack([entries[row_at, col_at] for col_at in range(5)]) for row_at in range(5)])
    matrix = 7.0 * (gram[:4, 1:] + gram[:4, :4])
    matrix = 0.5 * (matrix + matrix.T)
    return cholesky_solve(matrix, gram[:4, 0])

def update(solution, residual, basis, coeffs):
    for degree in range(4):
        solution = solution + coeffs[degree] * basis[degree]
        residual = residual - 7.0 * coeffs[degree] * (basis[degree + 1] + basis[degree])
    return (solution, residual)

def reference(right_side, diagonal, inlet_index, plate_order, conductance, plate_level):
    solution = jnp.zeros_like(right_side)
    residual = right_side
    for repeat in range(BLOCKS):
        basis = [residual]
        for degree in range(STEPS):
            padded = jnp.pad(basis[-1], ((1, 1), (1, 1), (0, 0)))
            basis.append(apply_shifted(padded, diagonal))
        gram_vec = jnp.stack([jnp.sum(basis[pair[0]] * basis[pair[1]]) for pair in GRAM_PAIRS])
        coeffs = solve_block(gram_vec)
        solution, residual = update(solution, residual, basis, coeffs)
    blocks = solution.reshape(N_SLAB, CZ, N_TILE, CY, NX).transpose(0, 2, 1, 3, 4).reshape(N_SLAB, N_TILE, CZ * CY * NX)
    picked = jnp.take_along_axis(blocks, inlet_index.reshape(N_SLAB, N_TILE, PLATES * INLETS).astype(jnp.int32), axis=2)
    contrib = lax.optimization_barrier(jnp.sum(picked.reshape(N_SLAB, N_TILE, PLATES, INLETS), axis=(0, 1, 3)))
    scale = 1.0 / jnp.sqrt(jnp.float32(N_SLAB * N_TILE * INLETS))
    header = jnp.take(contrib, plate_order, axis=0) * scale
    inlet_flow = conductance * (header - plate_level)
    return (solution, residual, inlet_flow)
```

```python
import functools

import jax
import jax.numpy as jnp
from jax import lax
from jax.experimental import pallas as pl
from jax.experimental.pallas import tpu as pltpu
from jax.sharding import PartitionSpec as P

STEPS = 4
HALO = 4
PAD = 8
MESH = pl.DeviceIdType.MESH
PAIRS = [(i, j) for i in range(5) for j in range(i, 5)]
DIRS = [(dz, dy) for dz in (-1, 0, 1) for dy in (-1, 0, 1) if (dz, dy) != (0, 0)]


def over(count, body):
    if count <= 16:
        for i in range(1, count):
            body(i)
    else:
        lax.fori_loop(1, count, lambda i, c: (body(i), c)[1], 0)


def solve4(m, g):
    m = [list(row) for row in m]
    g = list(g)
    inv = [None] * 4
    for k in range(4):
        inv[k] = 1.0 / m[k][k]
        for i in range(k + 1, 4):
            fac = m[i][k] * inv[k]
            for j in range(k + 1, i + 1):
                m[i][j] = m[i][j] - fac * m[j][k]
            g[i] = g[i] - fac * g[k]
    c = [None] * 4
    for k in range(3, -1, -1):
        value = g[k]
        for i in range(k + 1, 4):
            value = value - m[i][k] * c[i]
        c[k] = value * inv[k]
    return c


def coefficients(total):
    full = jnp.broadcast_to(jnp.sum(total, axis=1, keepdims=True), total.shape)
    gram = {}
    for at, (i, j) in enumerate(PAIRS):
        gram[i, j] = gram[j, i] = full[at : at + 1, :]
    m = [
        [
            3.5 * ((gram[i, j + 1] + gram[i, j]) + (gram[j, i + 1] + gram[j, i]))
            if j <= i
            else None
            for j in range(4)
        ]
        for i in range(4)
    ]
    return solve4(m, [gram[i, 0] for i in range(4)])


def kernel(
    n_slab, n_tile, rs, diag, index, order, conduct, level,
    sol, res, flow,
    ext, basis, ext2, basis2, dm, wt, first, msg1, part1, sum1, all1, msg2, part2, sum2, all2,
    h1s, h1r, h2s, h2r, a1s, a1r, b1s, b1r, a2s, a2r, b2s, b2r,
):
    cz, cy, nx = rs.shape
    plates, inlets = index.shape[2], index.shape[3]
    per = conduct.shape[0]
    me_s, me_t = lax.axis_index("slab"), lax.axis_index("tile")
    z_all, y_all = cz + 2 * HALO, cy + 2 * PAD
    own_z, own_y = slice(HALO, HALO + cz), slice(PAD, PAD + cy)

    ext[...] = jnp.zeros_like(ext)
    ext2[...] = jnp.zeros_like(ext2)
    ext[0, own_z, own_y, :] = rs[...]
    ext[1, own_z, own_y, :] = diag[...]

    barrier = pltpu.get_barrier_semaphore()

    def there(dz, dy):
        s, t = me_s + dz, me_t + dy
        return s, t, (s >= 0) & (s < n_slab) & (t >= 0) & (t < n_tile)

    for dz, dy in DIRS:
        if dz and dy:
            s, t, ok = there(dz, dy)

            @pl.when(ok)
            def _():
                pl.semaphore_signal(barrier, inc=1, device_id=(s, t), device_id_type=MESH)

    over(n_tile, lambda i: pl.semaphore_signal(
        barrier, inc=1, device_id=(me_s, lax.rem(me_t + i, n_tile)), device_id_type=MESH))
    over(n_slab, lambda i: pl.semaphore_signal(
        barrier, inc=1, device_id=(lax.rem(me_s + i, n_slab), me_t), device_id_type=MESH))
    beside_s = jnp.where(me_s > 0, 1, 0) + jnp.where(me_s < n_slab - 1, 1, 0)
    beside_t = jnp.where(me_t > 0, 1, 0) + jnp.where(me_t < n_tile - 1, 1, 0)
    pl.semaphore_wait(barrier, beside_s * beside_t + (n_tile - 1 + n_slab - 1))

    def halo_copy(ref, lead, at, send, recv):
        dz, dy = DIRS[at]
        src_z = {-1: slice(HALO, 2 * HALO), 0: own_z, 1: slice(cz, cz + HALO)}[dz]
        dst_z = {-1: slice(HALO + cz, z_all), 0: own_z, 1: slice(0, HALO)}[dz]
        src_y = {
            -1: slice(PAD, PAD + HALO), 0: own_y, 1: slice(PAD + cy - HALO, PAD + cy)
        }[dy]
        dst_y = {
            -1: slice(PAD + cy, PAD + cy + HALO), 0: own_y, 1: slice(PAD - HALO, PAD)
        }[dy]
        cut = lambda z, y: ref.at[lead + (pl.ds(z.start, z.stop - z.start), pl.ds(y.start, y.stop - y.start))]
        return pltpu.make_async_remote_copy(
            src_ref=cut(src_z, src_y), dst_ref=cut(dst_z, dst_y),
            send_sem=send.at[at], recv_sem=recv.at[at],
            device_id=(me_s + dz, me_t + dy), device_id_type=MESH,
        )

    def halo_start(ref, lead, send, recv):
        for at, (dz, dy) in enumerate(DIRS):

            @pl.when(there(dz, dy)[2])
            def _():
                halo_copy(ref, lead, at, send, recv).start()

    def halo_recv(ref, lead, send, recv):
        for at, (dz, dy) in enumerate(DIRS):

            @pl.when(there(-dz, -dy)[2])
            def _():
                halo_copy(ref, lead, at, send, recv).wait_recv()

    def halo_sent(ref, lead, send, recv):
        for at, (dz, dy) in enumerate(DIRS):

            @pl.when(there(dz, dy)[2])
            def _():
                halo_copy(ref, lead, at, send, recv).wait_send()

    halo_start(ext, (slice(None),), h1s, h1r)

    cells = index[0, 0]
    lanes = lax.broadcasted_iota(jnp.int32, (plates, nx), 1)
    hot = []
    for slot in range(inlets):
        where = jnp.broadcast_to(cells[:, slot : slot + 1], (plates, nx))
        line = jnp.where(where // nx == lanes, 1.0, 0.0).astype(jnp.bfloat16)
        hot.append(line)
    for slot in range(inlets):
        first[slot, :, 0:nx] = hot[slot]
        first[slot, :, nx:2 * nx] = hot[slot]

    for z in range(z_all):
        gz = me_s * cz + (z - HALO)
        gy = me_t * cy - PAD + lax.broadcasted_iota(jnp.int32, (y_all, nx), 0)
        inside = (gy >= 0) & (gy < n_tile * cy) & (gz >= 0) & (gz < n_slab * cz)
        wt[z] = jnp.where(inside, 1.0 / 7.0, 0.0)

    halo_recv(ext, (slice(None),), h1s, h1r)
    for z in range(z_all):
        dm[z] = (ext[1, z] - 1.0) * (1.0 / 7.0)

    lane_at = lax.broadcasted_iota(jnp.int32, (y_all, nx), 1)

    def powers(read, store):
        for k in range(STEPS):
            for z in range(k + 1, z_all - 1 - k):
                c = read(k, z)
                beside = read(k, z + 1) + read(k, z - 1)
                beside = beside + (pltpu.roll(c, 1, 0) + pltpu.roll(c, y_all - 1, 0))
                beside = beside + (
                    jnp.where(lane_at == 0, 0.0, pltpu.roll(c, 1, 1))
                    + jnp.where(lane_at == nx - 1, 0.0, pltpu.roll(c, nx - 1, 1))
                )
                store[k, z] = dm[z] * c - wt[z] * beside

    def products(own, msg):
        acc = [None] * len(PAIRS)
        for z in range(HALO, HALO + cz):
            v = [own(k, z) for k in range(5)]
            for at, (i, j) in enumerate(PAIRS):
                term = v[i] * v[j]
                acc[at] = term if acc[at] is None else acc[at] + term
        for at in range(len(PAIRS)):
            msg[at : at + 1, :] = jnp.sum(acc[at], axis=0, keepdims=True)
        msg[15:16, :] = jnp.zeros((1, nx), jnp.float32)

    def exchange(axis_at, count, msg, slots, send, recv):
        me = (me_s, me_t)[axis_at]

        def place(i):
            return lax.rem(me + i, count)

        def copy(to, slot):
            return pltpu.make_async_remote_copy(
                src_ref=msg, dst_ref=slots.at[slot],
                send_sem=send.at[to], recv_sem=recv.at[slot],
                device_id=(to, me_t) if axis_at == 0 else (me_s, to), device_id_type=MESH,
            )

        over(count, lambda i: copy(place(i), me).start())
        slots[me] = msg[...]
        over(count, lambda i: copy(place(i), place(i)).wait_recv())

        def sent():
            over(count, lambda i: copy(place(i), place(i)).wait_send())

        return sent

    def added(count, slots):
        if count <= 16:
            total = slots[0]
            for i in range(1, count):
                total = total + slots[i]
            return total
        return lax.fori_loop(1, count, lambda i, t: t + slots[i], slots[0])

    def read1(k, z):
        return ext[0, z] if k == 0 else basis[k - 1, z]

    def own1(k, z):
        return ext[0, z, own_y, :] if k == 0 else basis[k - 1, z, own_y, :]

    powers(read1, basis)
    products(own1, msg1)
    sent1 = exchange(1, n_tile, msg1, part1, a1s, a1r)
    sum1[...] = added(n_tile, part1)
    sent2 = exchange(0, n_slab, sum1, all1, b1s, b1r)
    c1 = coefficients(added(n_slab, all1))
    keep = [1.0 - 7.0 * c1[0]] + [-7.0 * (c1[k] + c1[k - 1]) for k in (1, 2, 3)] + [-7.0 * c1[3]]
    for z in range(HALO, HALO + cz):
        v = [own1(k, z) for k in range(5)]
        x = c1[0] * v[0]
        r = v[0]
        for k in range(4):
            if k:
                x = x + c1[k] * v[k]
            r = r - (7.0 * c1[k]) * (v[k + 1] + v[k])
        sol[z - HALO] = x
        ext2[z, own_y, :] = r
    halo_start(ext2, (), h2s, h2r)
    sent1()
    sent2()
    halo_sent(ext, (slice(None),), h1s, h1r)
    halo_recv(ext2, (), h2s, h2r)

    def read2(k, z):
        return ext2[z] if k == 0 else basis2[k - 1, z]

    def own2(k, z):
        return ext2[z, own_y, :] if k == 0 else basis2[k - 1, z, own_y, :]

    powers(read2, basis2)
    products(own2, msg2)

    fields = [jnp.concatenate([sol[z] for z in range(cz)], axis=0)] + [
        jnp.concatenate([own2(k, z) for z in range(HALO, HALO + cz)], axis=0) for k in range(4)
    ]
    table = jnp.zeros((plates, nx), jnp.float32)
    for at, field in enumerate(fields):
        high = field.astype(jnp.bfloat16)
        low = (field - high.astype(jnp.float32)).astype(jnp.bfloat16)
        both = jnp.concatenate([high, low], axis=0)
        total = None
        for slot in range(inlets):
            got = jnp.dot(first[slot], both, preferred_element_type=jnp.float32)
            where = jnp.broadcast_to(cells[:, slot : slot + 1], (plates, nx))
            got = jnp.where(where % nx == lanes, got, 0.0)
            total = got if total is None else total + got
        table = jnp.where(lanes == at, jnp.sum(total, axis=1, keepdims=True), table)
    msg2[16:, :] = table

    sent3 = exchange(1, n_tile, msg2, part2, a2s, a2r)
    sum2[...] = added(n_tile, part2)
    sent4 = exchange(0, n_slab, sum2, all2, b2s, b2r)
    everything = added(n_slab, all2)
    c2 = coefficients(everything[:16])
    for z in range(HALO, HALO + cz):
        v = [own2(k, z) for k in range(5)]
        x = sol[z - HALO]
        r = v[0]
        for k in range(4):
            x = x + c2[k] * v[k]
            r = r - (7.0 * c2[k]) * (v[k + 1] + v[k])
        sol[z - HALO] = x
        res[z - HALO] = r

    lane1 = lax.broadcasted_iota(jnp.int32, (1, nx), 1)
    mix = jnp.where(lane1 == 0, 1.0, 0.0)
    for k in range(4):
        mix = jnp.where(lane1 == k + 1, c2[k], mix)
    contrib = jnp.sum(everything[16:] * mix, axis=1, keepdims=True)
    contrib = jnp.broadcast_to(contrib, (plates, nx))
    plate_at = lax.broadcasted_iota(jnp.int32, (plates, nx), 0)
    scale = 1.0 / (float(n_slab * n_tile * inlets) ** 0.5)
    row = jnp.zeros((1, nx), jnp.float32)
    for j in range(per):
        spot = me_t * per + j
        header = jnp.sum(
            jnp.where(plate_at == order[spot], contrib, 0.0), axis=0, keepdims=True
        )
        row = jnp.where(lane1 == j, conduct[j] * (header * scale - level[j]), row)
    flow[...] = row[:, :per]

    sent3()
    sent4()
    halo_sent(ext2, (), h2s, h2r)


def on_device(n_slab, n_tile, right_side, diagonal, inlet_index, plate_order, conductance, plate_level):
    cz, cy, nx = right_side.shape
    plates, inlets = inlet_index.shape[2:]
    per = conductance.shape[0]
    z_all, y_all = cz + 2 * HALO, cy + 2 * PAD
    f32 = jnp.float32
    block = jax.ShapeDtypeStruct((cz, cy, nx), f32)
    vmem = pl.BlockSpec(memory_space=pltpu.VMEM)
    smem = pl.BlockSpec(memory_space=pltpu.SMEM)
    rows2 = 16 + plates
    dma = pltpu.SemaphoreType.DMA
    sol, res, flow = pl.pallas_call(
        functools.partial(kernel, n_slab, n_tile),
        out_shape=(block, block, jax.ShapeDtypeStruct((1, per), f32)),
        in_specs=[vmem, vmem, vmem, smem, smem, smem],
        out_specs=(vmem, vmem, vmem),
        scratch_shapes=[
            pltpu.VMEM((2, z_all, y_all, nx), f32),
            pltpu.VMEM((4, z_all, y_all, nx), f32),
            pltpu.VMEM((z_all, y_all, nx), f32),
            pltpu.VMEM((4, z_all, y_all, nx), f32),
            pltpu.VMEM((z_all, y_all, nx), f32),
            pltpu.VMEM((z_all, y_all, nx), f32),
            pltpu.VMEM((inlets, plates, 2 * nx), jnp.bfloat16),
            pltpu.VMEM((16, nx), f32),
            pltpu.VMEM((n_tile, 16, nx), f32),
            pltpu.VMEM((16, nx), f32),
            pltpu.VMEM((n_slab, 16, nx), f32),
            pltpu.VMEM((rows2, nx), f32),
            pltpu.VMEM((n_tile, rows2, nx), f32),
            pltpu.VMEM((rows2, nx), f32),
            pltpu.VMEM((n_slab, rows2, nx), f32),
            dma((8,)), dma((8,)), dma((8,)), dma((8,)),
            dma((n_tile,)), dma((n_tile,)), dma((n_slab,)), dma((n_slab,)),
            dma((n_tile,)), dma((n_tile,)), dma((n_slab,)), dma((n_slab,)),
        ],
        compiler_params=pltpu.CompilerParams(
            collective_id=0, has_side_effects=True, vmem_limit_bytes=48 * 1024 * 1024
        ),
    )(right_side, diagonal, inlet_index, plate_order, conductance, plate_level)
    return sol, res, flow.reshape(per)


def solution(mesh):
    in_specs = (
        P("slab", "tile", None),
        P("slab", "tile", None),
        P("slab", "tile", None, None),
        P(),
        P("tile"),
        P("tile"),
    )
    out_specs = (P("slab", "tile", None), P("slab", "tile", None), P("tile"))
    return jax.shard_map(
        functools.partial(on_device, mesh.shape["slab"], mesh.shape["tile"]),
        mesh=mesh, in_specs=in_specs, out_specs=out_specs, check_vma=False,
    )
```

```python
import functools

import jax
import jax.numpy as jnp
from jax import lax
from jax.experimental import pallas as pl
from jax.experimental.pallas import tpu as pltpu
from jax.sharding import PartitionSpec as P

STEPS = 4
HALO = 4
PAD = 8
MESH = pl.DeviceIdType.MESH
PAIRS = [(i, j) for i in range(5) for j in range(i, 5)]
ANY = pl.BlockSpec(memory_space=pl.ANY)
VMEM = pl.BlockSpec(memory_space=pltpu.VMEM)
DIRS = [(dz, dy) for dz in (-1, 0, 1) for dy in (-1, 0, 1) if (dz, dy) != (0, 0)]


def over(count, body):
    if count <= 32:
        for i in range(1, count):
            body(i)
    else:
        lax.fori_loop(1, count, lambda i, c: (body(i), c)[1], 0)


def solve4(m, g):
    m = [list(row) for row in m]
    g = list(g)
    inv = [None] * 4
    for k in range(4):
        inv[k] = 1.0 / m[k][k]
        for i in range(k + 1, 4):
            fac = m[i][k] * inv[k]
            for j in range(k + 1, i + 1):
                m[i][j] = m[i][j] - fac * m[j][k]
            g[i] = g[i] - fac * g[k]
    c = [None] * 4
    for k in range(3, -1, -1):
        value = g[k]
        for i in range(k + 1, 4):
            value = value - m[i][k] * c[i]
        c[k] = value * inv[k]
    return c


def to_lanes(column, at):
    sub = lax.broadcasted_iota(jnp.int32, column.shape, 0)
    lane = lax.broadcasted_iota(jnp.int32, column.shape, 1)
    return jnp.sum(jnp.where(lane + at == sub, column, 0.0), axis=0, keepdims=True)


def coefficients(row):
    sub = lax.broadcasted_iota(jnp.int32, (16, row.shape[1]), 0)
    lane = lax.broadcasted_iota(jnp.int32, (16, row.shape[1]), 1)
    full = jnp.sum(jnp.where(lane == sub, row, 0.0), axis=1, keepdims=True)
    full = jnp.broadcast_to(full, sub.shape)
    gram = {}
    for at, (i, j) in enumerate(PAIRS):
        gram[i, j] = gram[j, i] = full[at : at + 1, :]
    m = [
        [
            3.5 * ((gram[i, j + 1] + gram[i, j]) + (gram[j, i + 1] + gram[j, i]))
            if j <= i
            else None
            for j in range(4)
        ]
        for i in range(4)
    ]
    return solve4(m, [gram[i, 0] for i in range(4)])


def kernel(
    n_slab, n_tile, rs, diag, index, order_in, conduct_in, level_in,
    sol, res, flow,
    ext, basis, ext2, basis2, dm, wt, cells, first, here,
    order, conduct, level, msg1, part1, msg2, part2, msg3, part3,
    h1s, h1r, h2s, h2r, a1s, a1r, a2s, a2r, a3s, a3r, local,
):
    cz, cy, nx = rs.shape
    inlets, plates = index.shape[2], index.shape[3]
    per = conduct.shape[0]
    me_s, me_t = lax.axis_index("slab"), lax.axis_index("tile")
    count, me = n_slab * n_tile, me_s * n_tile + me_t
    z_all, y_all = cz + 2 * HALO, cy + 2 * PAD
    own_z, own_y = slice(HALO, HALO + cz), slice(PAD, PAD + cy)

    own = lambda lead: ext.at[lead, pl.ds(HALO, cz), pl.ds(PAD, cy)]
    loads = [
        pltpu.make_async_copy(src, dst, local.at[at])
        for at, (src, dst) in enumerate([
            (rs, own(0)), (diag, own(1)), (index.at[0, 0], cells),
            (order_in, order), (conduct_in, conduct), (level_in, level),
        ])
    ]
    ext[...] = jnp.zeros_like(ext)
    ext2[...] = jnp.zeros_like(ext2)
    for load in loads:
        load.start()

    barrier = pltpu.get_barrier_semaphore()

    def there(dz, dy):
        s, t = me_s + dz, me_t + dy
        return s, t, (s >= 0) & (s < n_slab) & (t >= 0) & (t < n_tile)

    def place(i):
        at = lax.rem(me + i, count)
        return at, (at // n_tile, lax.rem(at, n_tile))

    over(count, lambda i: pl.semaphore_signal(
        barrier, inc=1, device_id=place(i)[1], device_id_type=MESH))
    loads[0].wait()
    loads[1].wait()
    pl.semaphore_wait(barrier, count - 1)

    def halo_copy(ref, lead, at, send, recv):
        dz, dy = DIRS[at]
        src_z = {-1: slice(HALO, 2 * HALO), 0: own_z, 1: slice(cz, cz + HALO)}[dz]
        dst_z = {-1: slice(HALO + cz, z_all), 0: own_z, 1: slice(0, HALO)}[dz]
        src_y = {
            -1: slice(PAD, PAD + HALO), 0: own_y, 1: slice(PAD + cy - HALO, PAD + cy)
        }[dy]
        dst_y = {
            -1: slice(PAD + cy, PAD + cy + HALO), 0: own_y, 1: slice(PAD - HALO, PAD)
        }[dy]
        cut = lambda z, y: ref.at[lead + (pl.ds(z.start, z.stop - z.start), pl.ds(y.start, y.stop - y.start))]
        return pltpu.make_async_remote_copy(
            src_ref=cut(src_z, src_y), dst_ref=cut(dst_z, dst_y),
            send_sem=send.at[at], recv_sem=recv.at[at],
            device_id=(me_s + dz, me_t + dy), device_id_type=MESH,
        )

    def halo_start(ref, lead, send, recv):
        for at, (dz, dy) in enumerate(DIRS):

            @pl.when(there(dz, dy)[2])
            def _():
                halo_copy(ref, lead, at, send, recv).start()

    def halo_recv(ref, lead, send, recv):
        for at, (dz, dy) in enumerate(DIRS):

            @pl.when(there(-dz, -dy)[2])
            def _():
                halo_copy(ref, lead, at, send, recv).wait_recv()

    def halo_sent(ref, lead, send, recv):
        for at, (dz, dy) in enumerate(DIRS):

            @pl.when(there(dz, dy)[2])
            def _():
                halo_copy(ref, lead, at, send, recv).wait_send()

    halo_start(ext, (slice(None),), h1s, h1r)

    loads[2].wait()
    lanes = lax.broadcasted_iota(jnp.int32, (plates, nx), 1)
    padded = jnp.concatenate(
        [cells[...], jnp.zeros((nx - inlets, plates), jnp.int32)], axis=0
    )
    if plates % nx:
        padded = jnp.concatenate(
            [padded, jnp.zeros((nx, nx - plates % nx), jnp.int32)], axis=1
        )
    spots = jnp.concatenate(
        [padded[:, at : at + nx].T for at in range(0, padded.shape[1], nx)], axis=0
    )[:plates]
    for slot in range(inlets):
        where = jnp.broadcast_to(spots[:, slot : slot + 1], (plates, nx))
        line = jnp.where(where // nx == lanes, 1.0, 0.0).astype(jnp.bfloat16)
        first[slot] = jnp.concatenate([line, line], axis=1)
        here[slot] = jnp.where(where % nx == lanes, 1.0, 0.0)

    for z in range(z_all):
        gz = me_s * cz + (z - HALO)
        gy = me_t * cy - PAD + lax.broadcasted_iota(jnp.int32, (y_all, nx), 0)
        inside = (gy >= 0) & (gy < n_tile * cy) & (gz >= 0) & (gz < n_slab * cz)
        wt[z] = jnp.where(inside, 1.0 / 7.0, 0.0)

    halo_recv(ext, (slice(None),), h1s, h1r)
    for z in range(z_all):
        dm[z] = (ext[1, z] - 1.0) * (1.0 / 7.0)

    lane_at = lax.broadcasted_iota(jnp.int32, (y_all, nx), 1)

    def powers(read, store):
        for k in range(STEPS):
            for z in range(k + 1, z_all - 1 - k):
                c = read(k, z)
                beside = read(k, z + 1) + read(k, z - 1)
                beside = beside + (pltpu.roll(c, 1, 0) + pltpu.roll(c, y_all - 1, 0))
                beside = beside + (
                    jnp.where(lane_at == 0, 0.0, pltpu.roll(c, 1, 1))
                    + jnp.where(lane_at == nx - 1, 0.0, pltpu.roll(c, nx - 1, 1))
                )
                store[k, z] = dm[z] * c - wt[z] * beside

    def products(own, msg):
        acc = [None] * len(PAIRS)
        for z in range(HALO, HALO + cz):
            v = [own(k, z) for k in range(5)]
            for at, (i, j) in enumerate(PAIRS):
                term = v[i] * v[j]
                acc[at] = term if acc[at] is None else acc[at] + term
        rows = [jnp.sum(term, axis=0, keepdims=True) for term in acc]
        rows = jnp.concatenate(rows + [jnp.zeros((1, nx), jnp.float32)], axis=0)
        column = jnp.broadcast_to(jnp.sum(rows, axis=1, keepdims=True), rows.shape)
        msg[0:1, :] = to_lanes(column, 0)

    def inlet_sums(fields):
        halves = []
        for field in fields:
            high = field.astype(jnp.bfloat16)
            low = (field - high.astype(jnp.float32)).astype(jnp.bfloat16)
            halves.append(jnp.concatenate([high, low], axis=0))
        got = jnp.dot(
            first[...].reshape(inlets * plates, 2 * nx),
            jnp.concatenate(halves, axis=1),
            preferred_element_type=jnp.float32,
        )
        sums = []
        for at in range(len(fields)):
            total = None
            for slot in range(inlets):
                term = here[slot] * got[
                    slot * plates : (slot + 1) * plates, at * nx : (at + 1) * nx
                ]
                total = term if total is None else total + term
            total = jnp.sum(total, axis=1, keepdims=True)
            sums.append(jnp.broadcast_to(total, (plates, nx)))
        return sums

    def send(msg, slots, rows, send_sem, recv_sem):
        def copy(i):
            return pltpu.make_async_remote_copy(
                src_ref=msg.at[pl.ds(0, rows)], dst_ref=slots.at[me, pl.ds(0, rows)],
                send_sem=send_sem, recv_sem=recv_sem,
                device_id=place(i)[1], device_id_type=MESH,
            )

        others = slots.at[pl.ds(0, count - 1), pl.ds(0, rows)]
        every = pltpu.make_async_remote_copy(
            src_ref=others, dst_ref=others, send_sem=send_sem, recv_sem=recv_sem,
            device_id=place(1)[1], device_id_type=MESH,
        )
        over(count, lambda i: copy(i).start())
        slots[me, 0:rows, :] = msg[0:rows, :]

        def total():
            every.wait_recv()
            if count <= 32:
                parts = [slots[i, 0:rows, :] for i in range(count)]
                while len(parts) > 1:
                    parts = [
                        parts[i] + parts[i + 1] if i + 1 < len(parts) else parts[i]
                        for i in range(0, len(parts), 2)
                    ]
                return parts[0]
            return lax.fori_loop(
                1, count, lambda i, t: t + slots[i, 0:rows, :], slots[0, 0:rows, :]
            )

        return total, every.wait_send

    def read1(k, z):
        return ext[0, z] if k == 0 else basis[k - 1, z]

    def own1(k, z):
        return ext[0, z, own_y, :] if k == 0 else basis[k - 1, z, own_y, :]

    powers(read1, basis)
    products(own1, msg1)
    total1, sent1 = send(msg1, part1, 1, a1s, a1r)
    whole = lambda own, k: jnp.concatenate(
        [own(k, z) for z in range(HALO, HALO + cz)], axis=0
    )
    picked1 = inlet_sums([whole(own1, k) for k in range(4)])
    c1 = coefficients(total1())
    for z in range(HALO, HALO + cz):
        v = [own1(k, z) for k in range(5)]
        x = c1[0] * v[0]
        r = v[0]
        for k in range(4):
            if k:
                x = x + c1[k] * v[k]
            r = r - (7.0 * c1[k]) * (v[k + 1] + v[k])
        sol[z - HALO] = x
        ext2[z, own_y, :] = r
    halo_start(ext2, (), h2s, h2r)
    sent1()
    halo_sent(ext, (slice(None),), h1s, h1r)
    halo_recv(ext2, (), h2s, h2r)

    def read2(k, z):
        return ext2[z] if k == 0 else basis2[k - 1, z]

    def own2(k, z):
        return ext2[z, own_y, :] if k == 0 else basis2[k - 1, z, own_y, :]

    powers(read2, basis2)
    products(own2, msg2)
    total2, sent2 = send(msg2, part2, 1, a2s, a2r)

    so_far = picked1[0] * c1[0]
    for k in range(1, 4):
        so_far = so_far + picked1[k] * c1[k]
    picked2 = inlet_sums([whole(own2, k) for k in range(4)])
    blocks = part3.shape[1] // 8
    for at in range(blocks):
        for row, column in enumerate([so_far] + picked2):
            msg3[at * 8 + row : at * 8 + row + 1, :] = to_lanes(column, at * nx)
        msg3[at * 8 + 5 : at * 8 + 8, :] = jnp.zeros((3, nx), jnp.float32)
    total3, sent3 = send(msg3, part3, 8 * blocks, a3s, a3r)

    c2 = coefficients(total2())
    for z in range(HALO, HALO + cz):
        v = [own2(k, z) for k in range(5)]
        x = sol[z - HALO]
        r = v[0]
        for k in range(4):
            x = x + c2[k] * v[k]
            r = r - (7.0 * c2[k]) * (v[k + 1] + v[k])
        sol[z - HALO] = x
        res[z - HALO] = r

    lane1 = lax.broadcasted_iota(jnp.int32, (1, nx), 1)
    scale = 1.0 / (float(count * inlets) ** 0.5)
    sums = total3()
    contrib = []
    for at in range(blocks):
        value = sums[at * 8 : at * 8 + 1, :]
        for k in range(4):
            value = value + c2[k] * sums[at * 8 + 1 + k : at * 8 + 2 + k, :]
        contrib.append(value)
    for load in loads[3:]:
        load.wait()
    row = jnp.zeros((1, nx), jnp.float32)
    for j in range(per):
        plate = order[me_t * per + j]
        header = jnp.zeros((1, nx), jnp.float32)
        for at in range(blocks):
            header = header + jnp.where(lane1 + at * nx == plate, contrib[at], 0.0)
        header = jnp.sum(header, axis=1, keepdims=True)
        row = jnp.where(lane1 == j, conduct[j] * (header * scale - level[j]), row)
    flow[...] = row[:, :per]

    sent2()
    sent3()
    halo_sent(ext2, (), h2s, h2r)


def deliver(sol, res, flow, sol_out, res_out, flow_out, sems):
    copies = [
        pltpu.make_async_copy(src, dst, sems.at[at])
        for at, (src, dst) in enumerate([(sol, sol_out), (res, res_out), (flow, flow_out)])
    ]
    for copy in copies:
        copy.start()
    for copy in copies:
        copy.wait()


def on_device(n_slab, n_tile, right_side, diagonal, inlet_index, plate_order, conductance, plate_level):
    cz, cy, nx = right_side.shape
    inlet_index = inlet_index.transpose(0, 1, 3, 2)
    inlets, plates = inlet_index.shape[2:]
    per = conductance.shape[0]
    z_all, y_all = cz + 2 * HALO, cy + 2 * PAD
    count = n_slab * n_tile
    rows3 = 8 * -(-plates // nx)
    f32, i32 = jnp.float32, jnp.int32
    block = jax.ShapeDtypeStruct((cz, cy, nx), f32)
    shapes = (block, block, jax.ShapeDtypeStruct((1, per), f32))
    dma = pltpu.SemaphoreType.DMA
    results = pl.pallas_call(
        functools.partial(kernel, n_slab, n_tile),
        out_shape=tuple(pltpu.VMEM(leaf.shape, leaf.dtype) for leaf in shapes),
        in_specs=[ANY] * 6,
        out_specs=(VMEM,) * 3,
        scratch_shapes=[
            pltpu.VMEM((2, z_all, y_all, nx), f32),
            pltpu.VMEM((4, z_all, y_all, nx), f32),
            pltpu.VMEM((z_all, y_all, nx), f32),
            pltpu.VMEM((4, z_all, y_all, nx), f32),
            pltpu.VMEM((z_all, y_all, nx), f32),
            pltpu.VMEM((z_all, y_all, nx), f32),
            pltpu.VMEM((inlets, plates), i32),
            pltpu.VMEM((inlets, plates, 2 * nx), jnp.bfloat16),
            pltpu.VMEM((inlets, plates, nx), f32),
            pltpu.SMEM(plate_order.shape, i32),
            pltpu.SMEM((per,), f32),
            pltpu.SMEM((per,), f32),
            pltpu.VMEM((8, nx), f32),
            pltpu.VMEM((count, 8, nx), f32),
            pltpu.VMEM((8, nx), f32),
            pltpu.VMEM((count, 8, nx), f32),
            pltpu.VMEM((rows3, nx), f32),
            pltpu.VMEM((count, rows3, nx), f32),
            dma((8,)), dma((8,)), dma((8,)), dma((8,)),
            dma, dma, dma, dma, dma, dma, dma((6,)),
        ],
        compiler_params=pltpu.CompilerParams(
            collective_id=0, has_side_effects=True, vmem_limit_bytes=60 * 1024 * 1024
        ),
    )(right_side, diagonal, inlet_index, plate_order, conductance, plate_level)
    sol, res, flow = pl.pallas_call(
        deliver,
        out_shape=shapes,
        in_specs=[VMEM] * 3,
        out_specs=(ANY,) * 3,
        scratch_shapes=[dma((3,))],
    )(*results)
    return sol, res, flow.reshape(per)


def solution(mesh):
    in_specs = (
        P("slab", "tile", None),
        P("slab", "tile", None),
        P("slab", "tile", None, None),
        P(),
        P("tile"),
        P("tile"),
    )
    out_specs = (P("slab", "tile", None), P("slab", "tile", None), P("tile"))
    return jax.shard_map(
        functools.partial(on_device, mesh.shape["slab"], mesh.shape["tile"]),
        mesh=mesh, in_specs=in_specs, out_specs=out_specs, check_vma=False,
    )
```

```python
import functools

import jax
import jax.numpy as jnp
from jax import lax
from jax.experimental import pallas as pl
from jax.experimental.pallas import tpu as pltpu
from jax.sharding import PartitionSpec as P

STEPS = 4
HALO = 4
PAD = 8
MESH = pl.DeviceIdType.MESH
PAIRS = [(i, j) for i in range(5) for j in range(i, 5)]
ANY = pl.BlockSpec(memory_space=pl.ANY)
VMEM = pl.BlockSpec(memory_space=pltpu.VMEM)
DIRS = [(dz, dy) for dz in (-1, 0, 1) for dy in (-1, 0, 1) if (dz, dy) != (0, 0)]


def solve4(m, g):
    m = [list(row) for row in m]
    g = list(g)
    inv = [None] * 4
    for k in range(4):
        inv[k] = 1.0 / m[k][k]
        for i in range(k + 1, 4):
            fac = m[i][k] * inv[k]
            for j in range(k + 1, i + 1):
                m[i][j] = m[i][j] - fac * m[j][k]
            g[i] = g[i] - fac * g[k]
    c = [None] * 4
    for k in range(3, -1, -1):
        value = g[k]
        for i in range(k + 1, 4):
            value = value - m[i][k] * c[i]
        c[k] = value * inv[k]
    return c


def to_lanes(column, at):
    sub = lax.broadcasted_iota(jnp.int32, column.shape, 0)
    lane = lax.broadcasted_iota(jnp.int32, column.shape, 1)
    return jnp.sum(jnp.where(lane + at == sub, column, 0.0), axis=0, keepdims=True)


def coefficients(row):
    sub = lax.broadcasted_iota(jnp.int32, (16, row.shape[1]), 0)
    lane = lax.broadcasted_iota(jnp.int32, (16, row.shape[1]), 1)
    full = jnp.sum(jnp.where(lane == sub, row, 0.0), axis=1, keepdims=True)
    full = jnp.broadcast_to(full, sub.shape)
    gram = {}
    for at, (i, j) in enumerate(PAIRS):
        gram[i, j] = gram[j, i] = full[at : at + 1, :]
    m = [
        [
            3.5 * ((gram[i, j + 1] + gram[i, j]) + (gram[j, i + 1] + gram[j, i]))
            if j <= i
            else None
            for j in range(4)
        ]
        for i in range(4)
    ]
    return solve4(m, [gram[i, 0] for i in range(4)])


def kernel(
    n_slab, n_tile, rs, diag, index, order_in, conduct_in, level_in,
    sol, res, flow,
    ext, basis, ext2, basis2, dm, wt, cells, first, here,
    order, conduct, level, msg1, part1, msg2, part2, msg3, part3,
    h1s, h1r, h2s, h2r, a1s, a1r, a2s, a2r, a3s, a3r, local,
):
    cz, cy, nx = rs.shape
    inlets, plates = index.shape[2], index.shape[3]
    per = conduct.shape[0]
    me_s, me_t = lax.axis_index("slab"), lax.axis_index("tile")
    count, me = n_slab * n_tile, me_s * n_tile + me_t
    z_all, y_all = cz + 2 * HALO, cy + 2 * PAD
    own_z, own_y = slice(HALO, HALO + cz), slice(PAD, PAD + cy)

    def halo_cut(at):
        dz, dy = DIRS[at]
        wide = HALO - 1 if dz and dy else HALO
        src_z = {-1: slice(HALO, HALO + wide), 0: own_z, 1: slice(HALO + cz - wide, HALO + cz)}[dz]
        dst_z = {-1: slice(HALO + cz, HALO + cz + wide), 0: own_z, 1: slice(HALO - wide, HALO)}[dz]
        src_y = {-1: slice(PAD, PAD + wide), 0: own_y, 1: slice(PAD + cy - wide, PAD + cy)}[dy]
        dst_y = {-1: slice(PAD + cy, PAD + cy + wide), 0: own_y, 1: slice(PAD - wide, PAD)}[dy]
        return (src_z, src_y), (dst_z, dst_y)

    own = lambda lead: ext.at[lead, pl.ds(HALO, cz), pl.ds(PAD, cy)]
    loads = [
        pltpu.make_async_copy(src, dst, local.at[at])
        for at, (src, dst) in enumerate([
            (rs, own(0)), (diag, own(1)), (index.at[0, 0], cells),
            (order_in, order), (conduct_in, conduct), (level_in, level),
        ])
    ]
    for load in loads:
        load.start()

    barrier = pltpu.get_barrier_semaphore()

    def there(dz, dy):
        s, t = me_s + dz, me_t + dy
        return s, t, (s >= 0) & (s < n_slab) & (t >= 0) & (t < n_tile)

    def place(i):
        at = lax.rem(me + i, count)
        return lax.div(at, n_tile), lax.rem(at, n_tile)

    def every_other(body):
        if count <= 32:
            slabs = [lax.rem(me_s + i, n_slab) for i in range(n_slab)]
            tiles = [lax.rem(me_t + i, n_tile) for i in range(n_tile)]
            for j in range(n_tile):
                for i in range(n_slab):
                    if i or j:
                        body((slabs[i], tiles[j]))
        else:
            lax.fori_loop(1, count, lambda i, c: (body(place(i)), c)[1], 0)

    every_other(lambda device: pl.semaphore_signal(
        barrier, inc=1, device_id=device, device_id_type=MESH))

    for at, (dz, dy) in enumerate(DIRS):

        @pl.when(jnp.logical_not(there(-dz, -dy)[2]))
        def _():
            z, y = halo_cut(at)[1]
            ext[:, z, y, :] = jnp.zeros((2, z.stop - z.start, y.stop - y.start, nx), jnp.float32)
            ext2[z, y, :] = jnp.zeros((z.stop - z.start, y.stop - y.start, nx), jnp.float32)

    loads[0].wait()
    loads[1].wait()
    pl.semaphore_wait(barrier, count - 1)

    def halo_copy(ref, lead, at, send, recv):
        dz, dy = DIRS[at]
        src, dst = halo_cut(at)
        cut = lambda z, y: ref.at[
            lead + (pl.ds(z.start, z.stop - z.start), pl.ds(y.start, y.stop - y.start))
        ]
        return pltpu.make_async_remote_copy(
            src_ref=cut(*src), dst_ref=cut(*dst),
            send_sem=send.at[at], recv_sem=recv.at[at],
            device_id=(me_s + dz, me_t + dy), device_id_type=MESH,
        )

    def halo_start(ref, lead, send, recv):
        for at, (dz, dy) in enumerate(DIRS):

            @pl.when(there(dz, dy)[2])
            def _():
                halo_copy(ref, lead, at, send, recv).start()

    def halo_recv(ref, lead, send, recv):
        for at, (dz, dy) in enumerate(DIRS):

            @pl.when(there(-dz, -dy)[2])
            def _():
                halo_copy(ref, lead, at, send, recv).wait_recv()

    def halo_sent(ref, lead, send, recv):
        for at, (dz, dy) in enumerate(DIRS):

            @pl.when(there(dz, dy)[2])
            def _():
                halo_copy(ref, lead, at, send, recv).wait_send()

    halo_start(ext, (slice(None),), h1s, h1r)

    loads[2].wait()
    lanes = lax.broadcasted_iota(jnp.int32, (plates, nx), 1)
    padded = jnp.concatenate(
        [cells[...], jnp.zeros((nx - inlets, plates), jnp.int32)], axis=0
    )
    if plates % nx:
        padded = jnp.concatenate(
            [padded, jnp.zeros((nx, nx - plates % nx), jnp.int32)], axis=1
        )
    spots = jnp.concatenate(
        [padded[:, at : at + nx].T for at in range(0, padded.shape[1], nx)], axis=0
    )[:plates]
    for slot in range(inlets):
        where = jnp.broadcast_to(spots[:, slot : slot + 1], (plates, nx))
        line = jnp.where(where // nx == lanes, 1.0, 0.0).astype(jnp.bfloat16)
        first[slot] = jnp.concatenate([line, line], axis=1)
        here[slot] = jnp.where(where % nx == lanes, 1.0, 0.0)

    for z in range(z_all):
        gz = me_s * cz + (z - HALO)
        gy = me_t * cy - PAD + lax.broadcasted_iota(jnp.int32, (y_all, nx), 0)
        inside = (gy >= 0) & (gy < n_tile * cy) & (gz >= 0) & (gz < n_slab * cz)
        wt[z] = jnp.where(inside, 1.0 / 7.0, 0.0)

    halo_recv(ext, (slice(None),), h1s, h1r)
    for z in range(z_all):
        dm[z] = (ext[1, z] - 1.0) * (1.0 / 7.0)

    lane_at = lax.broadcasted_iota(jnp.int32, (y_all, nx), 1)

    def powers(read, store):
        for k in range(STEPS):
            for z in range(k + 1, z_all - 1 - k):
                c = read(k, z)
                beside = read(k, z + 1) + read(k, z - 1)
                beside = beside + (pltpu.roll(c, 1, 0) + pltpu.roll(c, y_all - 1, 0))
                beside = beside + (
                    jnp.where(lane_at == 0, 0.0, pltpu.roll(c, 1, 1))
                    + jnp.where(lane_at == nx - 1, 0.0, pltpu.roll(c, nx - 1, 1))
                )
                store[k, z] = dm[z] * c - wt[z] * beside

    def products(own, msg):
        acc = [None] * len(PAIRS)
        for z in range(HALO, HALO + cz):
            v = [own(k, z) for k in range(5)]
            for at, (i, j) in enumerate(PAIRS):
                term = v[i] * v[j]
                acc[at] = term if acc[at] is None else acc[at] + term
        rows = [jnp.sum(term, axis=0, keepdims=True) for term in acc]
        rows = jnp.concatenate(rows + [jnp.zeros((1, nx), jnp.float32)], axis=0)
        column = jnp.broadcast_to(jnp.sum(rows, axis=1, keepdims=True), rows.shape)
        msg[0:1, :] = to_lanes(column, 0)

    def inlet_sums(fields):
        halves = []
        for field in fields:
            high = field.astype(jnp.bfloat16)
            low = (field - high.astype(jnp.float32)).astype(jnp.bfloat16)
            halves.append(jnp.concatenate([high, low], axis=0))
        got = jnp.dot(
            first[...].reshape(inlets * plates, 2 * nx),
            jnp.concatenate(halves, axis=1),
            preferred_element_type=jnp.float32,
        )
        sums = []
        for at in range(len(fields)):
            total = None
            for slot in range(inlets):
                term = here[slot] * got[
                    slot * plates : (slot + 1) * plates, at * nx : (at + 1) * nx
                ]
                total = term if total is None else total + term
            total = jnp.sum(total, axis=1, keepdims=True)
            sums.append(jnp.broadcast_to(total, (plates, nx)))
        return sums

    def send(msg, slots, rows, send_sem, recv_sem):
        def copy(device):
            return pltpu.make_async_remote_copy(
                src_ref=msg.at[pl.ds(0, rows)], dst_ref=slots.at[me, pl.ds(0, rows)],
                send_sem=send_sem, recv_sem=recv_sem,
                device_id=device, device_id_type=MESH,
            )

        others = slots.at[pl.ds(0, count - 1), pl.ds(0, rows)]
        every = pltpu.make_async_remote_copy(
            src_ref=others, dst_ref=others, send_sem=send_sem, recv_sem=recv_sem,
            device_id=place(1), device_id_type=MESH,
        )
        every_other(lambda device: copy(device).start())
        slots[me, 0:rows, :] = msg[0:rows, :]

        def total():
            every.wait_recv()
            if count <= 32:
                parts = [slots[i, 0:rows, :] for i in range(count)]
                while len(parts) > 1:
                    parts = [
                        parts[i] + parts[i + 1] if i + 1 < len(parts) else parts[i]
                        for i in range(0, len(parts), 2)
                    ]
                return parts[0]
            return lax.fori_loop(
                1, count, lambda i, t: t + slots[i, 0:rows, :], slots[0, 0:rows, :]
            )

        return total, every.wait_send

    def read1(k, z):
        return ext[0, z] if k == 0 else basis[k - 1, z]

    def own1(k, z):
        return ext[0, z, own_y, :] if k == 0 else basis[k - 1, z, own_y, :]

    powers(read1, basis)
    products(own1, msg1)
    total1, sent1 = send(msg1, part1, 1, a1s, a1r)
    whole = lambda own, k: jnp.concatenate(
        [own(k, z) for z in range(HALO, HALO + cz)], axis=0
    )
    picked1 = inlet_sums([whole(own1, k) for k in range(4)])
    c1 = coefficients(total1())
    for z in range(HALO, HALO + cz):
        v = [own1(k, z) for k in range(5)]
        x = c1[0] * v[0]
        r = v[0]
        for k in range(4):
            if k:
                x = x + c1[k] * v[k]
            r = r - (7.0 * c1[k]) * (v[k + 1] + v[k])
        sol[z - HALO] = x
        ext2[z, own_y, :] = r
    halo_start(ext2, (), h2s, h2r)
    sent1()
    halo_sent(ext, (slice(None),), h1s, h1r)
    halo_recv(ext2, (), h2s, h2r)

    def read2(k, z):
        return ext2[z] if k == 0 else basis2[k - 1, z]

    def own2(k, z):
        return ext2[z, own_y, :] if k == 0 else basis2[k - 1, z, own_y, :]

    powers(read2, basis2)
    products(own2, msg2)
    total2, sent2 = send(msg2, part2, 1, a2s, a2r)

    so_far = picked1[0] * c1[0]
    for k in range(1, 4):
        so_far = so_far + picked1[k] * c1[k]
    picked2 = inlet_sums([whole(own2, k) for k in range(4)])
    blocks = part3.shape[1] // 8
    for at in range(blocks):
        for row, column in enumerate([so_far] + picked2):
            msg3[at * 8 + row : at * 8 + row + 1, :] = to_lanes(column, at * nx)
        msg3[at * 8 + 5 : at * 8 + 8, :] = jnp.zeros((3, nx), jnp.float32)
    total3, sent3 = send(msg3, part3, 8 * blocks, a3s, a3r)

    c2 = coefficients(total2())
    for z in range(HALO, HALO + cz):
        v = [own2(k, z) for k in range(5)]
        x = sol[z - HALO]
        r = v[0]
        for k in range(4):
            x = x + c2[k] * v[k]
            r = r - (7.0 * c2[k]) * (v[k + 1] + v[k])
        sol[z - HALO] = x
        res[z - HALO] = r

    lane1 = lax.broadcasted_iota(jnp.int32, (1, nx), 1)
    scale = 1.0 / (float(count * inlets) ** 0.5)
    sums = total3()
    contrib = []
    for at in range(blocks):
        value = sums[at * 8 : at * 8 + 1, :]
        for k in range(4):
            value = value + c2[k] * sums[at * 8 + 1 + k : at * 8 + 2 + k, :]
        contrib.append(value)
    for load in loads[3:]:
        load.wait()
    row = jnp.zeros((1, nx), jnp.float32)
    for j in range(per):
        plate = order[me_t * per + j]
        header = jnp.zeros((1, nx), jnp.float32)
        for at in range(blocks):
            header = header + jnp.where(lane1 + at * nx == plate, contrib[at], 0.0)
        header = jnp.sum(header, axis=1, keepdims=True)
        row = jnp.where(lane1 == j, conduct[j] * (header * scale - level[j]), row)
    flow[...] = row[:, :per]

    sent2()
    sent3()
    halo_sent(ext2, (), h2s, h2r)


def deliver(sol, res, flow, sol_out, res_out, flow_out, sems):
    copies = [
        pltpu.make_async_copy(src, dst, sems.at[at])
        for at, (src, dst) in enumerate([(sol, sol_out), (res, res_out), (flow, flow_out)])
    ]
    for copy in copies:
        copy.start()
    for copy in copies:
        copy.wait()


def on_device(n_slab, n_tile, right_side, diagonal, inlet_index, plate_order, conductance, plate_level):
    cz, cy, nx = right_side.shape
    inlet_index = inlet_index.transpose(0, 1, 3, 2)
    inlets, plates = inlet_index.shape[2:]
    per = conductance.shape[0]
    z_all, y_all = cz + 2 * HALO, cy + 2 * PAD
    count = n_slab * n_tile
    rows3 = 8 * -(-plates // nx)
    f32, i32 = jnp.float32, jnp.int32
    block = jax.ShapeDtypeStruct((cz, cy, nx), f32)
    shapes = (block, block, jax.ShapeDtypeStruct((1, per), f32))
    dma = pltpu.SemaphoreType.DMA
    results = pl.pallas_call(
        functools.partial(kernel, n_slab, n_tile),
        out_shape=tuple(pltpu.VMEM(leaf.shape, leaf.dtype) for leaf in shapes),
        in_specs=[ANY] * 6,
        out_specs=(VMEM,) * 3,
        scratch_shapes=[
            pltpu.VMEM((2, z_all, y_all, nx), f32),
            pltpu.VMEM((4, z_all, y_all, nx), f32),
            pltpu.VMEM((z_all, y_all, nx), f32),
            pltpu.VMEM((4, z_all, y_all, nx), f32),
            pltpu.VMEM((z_all, y_all, nx), f32),
            pltpu.VMEM((z_all, y_all, nx), f32),
            pltpu.VMEM((inlets, plates), i32),
            pltpu.VMEM((inlets, plates, 2 * nx), jnp.bfloat16),
            pltpu.VMEM((inlets, plates, nx), f32),
            pltpu.SMEM(plate_order.shape, i32),
            pltpu.SMEM((per,), f32),
            pltpu.SMEM((per,), f32),
            pltpu.VMEM((8, nx), f32),
            pltpu.VMEM((count, 8, nx), f32),
            pltpu.VMEM((8, nx), f32),
            pltpu.VMEM((count, 8, nx), f32),
            pltpu.VMEM((rows3, nx), f32),
            pltpu.VMEM((count, rows3, nx), f32),
            dma((8,)), dma((8,)), dma((8,)), dma((8,)),
            dma, dma, dma, dma, dma, dma, dma((6,)),
        ],
        compiler_params=pltpu.CompilerParams(
            collective_id=0, has_side_effects=True, vmem_limit_bytes=60 * 1024 * 1024
        ),
    )(right_side, diagonal, inlet_index, plate_order, conductance, plate_level)
    sol, res, flow = pl.pallas_call(
        deliver,
        out_shape=shapes,
        in_specs=[VMEM] * 3,
        out_specs=(ANY,) * 3,
        scratch_shapes=[dma((3,))],
        compiler_params=pltpu.CompilerParams(vmem_limit_bytes=1024 * 1024),
    )(*results)
    return sol, res, flow.reshape(per)


def solution(mesh):
    in_specs = (
        P("slab", "tile", None),
        P("slab", "tile", None),
        P("slab", "tile", None, None),
        P(),
        P("tile"),
        P("tile"),
    )
    out_specs = (P("slab", "tile", None), P("slab", "tile", None), P("tile"))
    return jax.shard_map(
        functools.partial(on_device, mesh.shape["slab"], mesh.shape["tile"]),
        mesh=mesh, in_specs=in_specs, out_specs=out_specs, check_vma=False,
    )
```

```python
import functools

import jax
import jax.numpy as jnp
from jax import lax
from jax.experimental import pallas as pl
from jax.experimental.pallas import tpu as pltpu
from jax.sharding import PartitionSpec as P

STEPS = 4
HALO = 4
PAD = 8
MESH = pl.DeviceIdType.MESH
PAIRS = [(i, j) for i in range(5) for j in range(i, 5)]
ANY = pl.BlockSpec(memory_space=pl.ANY)
VMEM = pl.BlockSpec(memory_space=pltpu.VMEM)
DIRS = [(dz, dy) for dz in (-1, 0, 1) for dy in (-1, 0, 1) if (dz, dy) != (0, 0)]


def solve4(m, g):
    m = [list(row) for row in m]
    g = list(g)
    inv = [None] * 4
    for k in range(4):
        inv[k] = 1.0 / m[k][k]
        for i in range(k + 1, 4):
            fac = m[i][k] * inv[k]
            for j in range(k + 1, i + 1):
                m[i][j] = m[i][j] - fac * m[j][k]
            g[i] = g[i] - fac * g[k]
    c = [None] * 4
    for k in range(3, -1, -1):
        value = g[k]
        for i in range(k + 1, 4):
            value = value - m[i][k] * c[i]
        c[k] = value * inv[k]
    return c


def to_lanes(column, at):
    sub = lax.broadcasted_iota(jnp.int32, column.shape, 0)
    lane = lax.broadcasted_iota(jnp.int32, column.shape, 1)
    return jnp.sum(jnp.where(lane + at == sub, column, 0.0), axis=0, keepdims=True)


def coefficients(row):
    sub = lax.broadcasted_iota(jnp.int32, (16, row.shape[1]), 0)
    lane = lax.broadcasted_iota(jnp.int32, (16, row.shape[1]), 1)
    full = jnp.sum(jnp.where(lane == sub, row, 0.0), axis=1, keepdims=True)
    full = jnp.broadcast_to(full, sub.shape)
    gram = {}
    for at, (i, j) in enumerate(PAIRS):
        gram[i, j] = gram[j, i] = full[at : at + 1, :]
    m = [
        [
            3.5 * ((gram[i, j + 1] + gram[i, j]) + (gram[j, i + 1] + gram[j, i]))
            if j <= i
            else None
            for j in range(4)
        ]
        for i in range(4)
    ]
    return solve4(m, [gram[i, 0] for i in range(4)])


def kernel(
    n_slab, n_tile, rs, diag, index, order_in, conduct_in, level_in,
    sol, res, flow,
    ext, basis, dm, wt, cells, first, here, coeffs,
    order, conduct, level, msg1, part1, msg2, part2,
    h1s, h1r, h2s, h2r, a1s, a1r, a2s, a2r, local,
):
    cz, cy, nx = rs.shape
    inlets, plates = index.shape[2], index.shape[3]
    per = conduct.shape[0]
    me_s, me_t = lax.axis_index("slab"), lax.axis_index("tile")
    count, me = n_slab * n_tile, me_s * n_tile + me_t
    z_all, y_all = cz + 2 * HALO, cy + 2 * PAD
    own_z, own_y = slice(HALO, HALO + cz), slice(PAD, PAD + cy)

    def halo_cut(at):
        dz, dy = DIRS[at]
        wide = HALO - 1 if dz and dy else HALO
        src_z = {-1: slice(HALO, HALO + wide), 0: own_z, 1: slice(HALO + cz - wide, HALO + cz)}[dz]
        dst_z = {-1: slice(HALO + cz, HALO + cz + wide), 0: own_z, 1: slice(HALO - wide, HALO)}[dz]
        src_y = {-1: slice(PAD, PAD + wide), 0: own_y, 1: slice(PAD + cy - wide, PAD + cy)}[dy]
        dst_y = {-1: slice(PAD + cy, PAD + cy + wide), 0: own_y, 1: slice(PAD - wide, PAD)}[dy]
        return (src_z, src_y), (dst_z, dst_y)

    own = lambda lead: ext.at[lead, pl.ds(HALO, cz), pl.ds(PAD, cy)]
    loads = [
        pltpu.make_async_copy(src, dst, local.at[at])
        for at, (src, dst) in enumerate([
            (rs, own(0)), (diag, own(1)), (index.at[0, 0], cells),
            (order_in, order), (conduct_in, conduct), (level_in, level),
        ])
    ]
    for load in loads:
        load.start()

    barrier = pltpu.get_barrier_semaphore()

    def there(dz, dy):
        s, t = me_s + dz, me_t + dy
        return s, t, (s >= 0) & (s < n_slab) & (t >= 0) & (t < n_tile)

    def place(i):
        at = lax.rem(me + i, count)
        return lax.div(at, n_tile), lax.rem(at, n_tile)

    def every_other(body):
        if count <= 32:
            slabs = [lax.rem(me_s + i, n_slab) for i in range(n_slab)]
            tiles = [lax.rem(me_t + i, n_tile) for i in range(n_tile)]
            for j in range(n_tile):
                for i in range(n_slab):
                    if i or j:
                        body((slabs[i], tiles[j]))
        else:
            lax.fori_loop(1, count, lambda i, c: (body(place(i)), c)[1], 0)

    every_other(lambda device: pl.semaphore_signal(
        barrier, inc=1, device_id=device, device_id_type=MESH))

    for at, (dz, dy) in enumerate(DIRS):

        @pl.when(jnp.logical_not(there(-dz, -dy)[2]))
        def _():
            z, y = halo_cut(at)[1]
            ext[:, z, y, :] = jnp.zeros((3, z.stop - z.start, y.stop - y.start, nx), jnp.float32)

    loads[0].wait()
    loads[1].wait()
    pl.semaphore_wait(barrier, count - 1)

    def halo_copy(ref, lead, at, send, recv):
        dz, dy = DIRS[at]
        src, dst = halo_cut(at)
        cut = lambda z, y: ref.at[
            lead + (pl.ds(z.start, z.stop - z.start), pl.ds(y.start, y.stop - y.start))
        ]
        return pltpu.make_async_remote_copy(
            src_ref=cut(*src), dst_ref=cut(*dst),
            send_sem=send.at[at], recv_sem=recv.at[at],
            device_id=(me_s + dz, me_t + dy), device_id_type=MESH,
        )

    def halo_start(ref, lead, send, recv):
        for at, (dz, dy) in enumerate(DIRS):

            @pl.when(there(dz, dy)[2])
            def _():
                halo_copy(ref, lead, at, send, recv).start()

    def halo_recv(ref, lead, send, recv):
        for at, (dz, dy) in enumerate(DIRS):

            @pl.when(there(-dz, -dy)[2])
            def _():
                halo_copy(ref, lead, at, send, recv).wait_recv()

    def halo_sent(ref, lead, send, recv):
        for at, (dz, dy) in enumerate(DIRS):

            @pl.when(there(dz, dy)[2])
            def _():
                halo_copy(ref, lead, at, send, recv).wait_send()

    halo_start(ext, (pl.ds(0, 2),), h1s, h1r)

    loads[2].wait()
    lanes = lax.broadcasted_iota(jnp.int32, (plates, nx), 1)
    padded = jnp.concatenate(
        [cells[...], jnp.zeros((nx - inlets, plates), jnp.int32)], axis=0
    )
    if plates % nx:
        padded = jnp.concatenate(
            [padded, jnp.zeros((nx, nx - plates % nx), jnp.int32)], axis=1
        )
    spots = jnp.concatenate(
        [padded[:, at : at + nx].T for at in range(0, padded.shape[1], nx)], axis=0
    )[:plates]
    for slot in range(inlets):
        where = jnp.broadcast_to(spots[:, slot : slot + 1], (plates, nx))
        line = jnp.where(where // nx == lanes, 1.0, 0.0).astype(jnp.bfloat16)
        first[slot] = jnp.concatenate([line, line], axis=1)
        here[slot] = jnp.where(where % nx == lanes, 1.0, 0.0)

    for z in range(z_all):
        gz = me_s * cz + (z - HALO)
        gy = me_t * cy - PAD + lax.broadcasted_iota(jnp.int32, (y_all, nx), 0)
        inside = (gy >= 0) & (gy < n_tile * cy) & (gz >= 0) & (gz < n_slab * cz)
        wt[z] = jnp.where(inside, 1.0 / 7.0, 0.0)

    halo_recv(ext, (pl.ds(0, 2),), h1s, h1r)
    for z in range(z_all):
        dm[z] = (ext[1, z] - 1.0) * (1.0 / 7.0)

    lane_at = lax.broadcasted_iota(jnp.int32, (y_all, nx), 1)

    def powers(read, store):
        for k in range(STEPS):
            for z in range(k + 1, z_all - 1 - k):
                c = read(k, z)
                beside = read(k, z + 1) + read(k, z - 1)
                beside = beside + (pltpu.roll(c, 1, 0) + pltpu.roll(c, y_all - 1, 0))
                beside = beside + (
                    jnp.where(lane_at == 0, 0.0, pltpu.roll(c, 1, 1))
                    + jnp.where(lane_at == nx - 1, 0.0, pltpu.roll(c, nx - 1, 1))
                )
                store[k, z] = dm[z] * c - wt[z] * beside

    def products(own):
        acc = [None] * len(PAIRS)
        for z in range(HALO, HALO + cz):
            v = [own(k, z) for k in range(5)]
            for at, (i, j) in enumerate(PAIRS):
                term = v[i] * v[j]
                acc[at] = term if acc[at] is None else acc[at] + term
        rows = [jnp.sum(term, axis=0, keepdims=True) for term in acc]
        rows = jnp.concatenate(rows + [jnp.zeros((1, nx), jnp.float32)], axis=0)
        column = jnp.broadcast_to(jnp.sum(rows, axis=1, keepdims=True), rows.shape)
        return to_lanes(column, 0)

    def inlet_sums(fields):
        halves = []
        for field in fields:
            high = field.astype(jnp.bfloat16)
            low = (field - high.astype(jnp.float32)).astype(jnp.bfloat16)
            halves.append(jnp.concatenate([high, low], axis=0))
        got = jnp.dot(
            first[...].reshape(inlets * plates, 2 * nx),
            jnp.concatenate(halves, axis=1),
            preferred_element_type=jnp.float32,
        )
        sums = []
        for at in range(len(fields)):
            total = None
            for slot in range(inlets):
                term = here[slot] * got[
                    slot * plates : (slot + 1) * plates, at * nx : (at + 1) * nx
                ]
                total = term if total is None else total + term
            total = jnp.sum(total, axis=1, keepdims=True)
            sums.append(jnp.broadcast_to(total, (plates, nx)))
        return sums

    def send(msg, slots, at, rows, send_sem, recv_sem):
        send_sem, recv_sem = send_sem.at[at], recv_sem.at[at]

        def copy(device):
            return pltpu.make_async_remote_copy(
                src_ref=msg.at[at, pl.ds(0, rows)], dst_ref=slots.at[at, me, pl.ds(0, rows)],
                send_sem=send_sem, recv_sem=recv_sem,
                device_id=device, device_id_type=MESH,
            )

        others = slots.at[at, pl.ds(0, count - 1), pl.ds(0, rows)]
        every = pltpu.make_async_remote_copy(
            src_ref=others, dst_ref=others, send_sem=send_sem, recv_sem=recv_sem,
            device_id=place(1), device_id_type=MESH,
        )
        def start():
            every_other(lambda device: copy(device).start())
            slots[at, me, 0:rows, :] = msg[at, 0:rows, :]

        def total():
            every.wait_recv()
            if count <= 32:
                parts = [slots[at, i, 0:rows, :] for i in range(count)]
                while len(parts) > 1:
                    parts = [
                        parts[i] + parts[i + 1] if i + 1 < len(parts) else parts[i]
                        for i in range(0, len(parts), 2)
                    ]
                return parts[0]
            return lax.fori_loop(
                1, count, lambda i, t: t + slots[at, i, 0:rows, :], slots[at, 0, 0:rows, :]
            )

        return start, total, every.wait_send

    blocks = -(-plates // nx)
    grams = lambda at: send(msg1, part1, at, 1, a1s, a1r)
    inlet = lambda at: send(msg2, part2, at, 4 * blocks, a2s, a2r)
    sol[...] = jnp.zeros_like(sol)

    def one_block(repeat, carry):
        v0 = 2 * repeat

        def read(k, z):
            return ext[v0, z] if k == 0 else basis[k - 1, z]

        def own(k, z):
            return ext[v0, z, own_y, :] if k == 0 else basis[k - 1, z, own_y, :]

        powers(read, basis)
        msg1[repeat, 0:1, :] = products(own)
        start, total, _ = grams(repeat)
        start()

        picked = inlet_sums([
            jnp.concatenate([own(k, z) for z in range(HALO, HALO + cz)], axis=0)
            for k in range(4)
        ])
        for k, column in enumerate(picked):
            for at in range(blocks):
                row = k * blocks + at
                msg2[repeat, row : row + 1, :] = to_lanes(column, at * nx)
        inlet(repeat)[0]()

        c = coefficients(total())
        for k in range(4):
            coeffs[repeat, k : k + 1, :] = c[k]
        for z in range(HALO, HALO + cz):
            v = [own(k, z) for k in range(5)]
            x = sol[z - HALO]
            r = v[0]
            for k in range(4):
                x = x + c[k] * v[k]
                r = r - (7.0 * c[k]) * (v[k + 1] + v[k])
            sol[z - HALO] = x
            res[z - HALO] = r

        @pl.when(repeat == 0)
        def _():
            ext[2, own_z, own_y, :] = res[...]
            halo_start(ext, (2,), h2s, h2r)
            halo_recv(ext, (2,), h2s, h2r)

        return carry

    lax.fori_loop(0, 2, one_block, 0)

    lane1 = lax.broadcasted_iota(jnp.int32, (1, nx), 1)
    scale = 1.0 / (float(count * inlets) ** 0.5)
    contrib = [0.0] * blocks
    for repeat in range(2):
        sums = inlet(repeat)[1]()
        for k in range(4):
            for at in range(blocks):
                row = k * blocks + at
                contrib[at] = (
                    contrib[at] + coeffs[repeat, k : k + 1, :] * sums[row : row + 1, :]
                )
    for load in loads[3:]:
        load.wait()
    row = jnp.zeros((1, nx), jnp.float32)
    for j in range(per):
        plate = order[me_t * per + j]
        header = jnp.zeros((1, nx), jnp.float32)
        for at in range(blocks):
            header = header + jnp.where(lane1 + at * nx == plate, contrib[at], 0.0)
        header = jnp.sum(header, axis=1, keepdims=True)
        row = jnp.where(lane1 == j, conduct[j] * (header * scale - level[j]), row)
    flow[...] = row[:, :per]

    for repeat in range(2):
        grams(repeat)[2]()
        inlet(repeat)[2]()
    halo_sent(ext, (pl.ds(0, 2),), h1s, h1r)
    halo_sent(ext, (2,), h2s, h2r)


def deliver(sol, res, flow, sol_out, res_out, flow_out, sems):
    copies = [
        pltpu.make_async_copy(src, dst, sems.at[at])
        for at, (src, dst) in enumerate([(sol, sol_out), (res, res_out), (flow, flow_out)])
    ]
    for copy in copies:
        copy.start()
    for copy in copies:
        copy.wait()


def on_device(n_slab, n_tile, right_side, diagonal, inlet_index, plate_order, conductance, plate_level):
    cz, cy, nx = right_side.shape
    inlet_index = inlet_index.transpose(0, 1, 3, 2)
    inlets, plates = inlet_index.shape[2:]
    per = conductance.shape[0]
    z_all, y_all = cz + 2 * HALO, cy + 2 * PAD
    count = n_slab * n_tile
    rows2 = 8 * -(-4 * -(-plates // nx) // 8)
    f32, i32 = jnp.float32, jnp.int32
    block = jax.ShapeDtypeStruct((cz, cy, nx), f32)
    shapes = (block, block, jax.ShapeDtypeStruct((1, per), f32))
    dma = pltpu.SemaphoreType.DMA
    results = pl.pallas_call(
        functools.partial(kernel, n_slab, n_tile),
        out_shape=tuple(pltpu.VMEM(leaf.shape, leaf.dtype) for leaf in shapes),
        in_specs=[ANY] * 6,
        out_specs=(VMEM,) * 3,
        scratch_shapes=[
            pltpu.VMEM((3, z_all, y_all, nx), f32),
            pltpu.VMEM((4, z_all, y_all, nx), f32),
            pltpu.VMEM((z_all, y_all, nx), f32),
            pltpu.VMEM((z_all, y_all, nx), f32),
            pltpu.VMEM((inlets, plates), i32),
            pltpu.VMEM((inlets, plates, 2 * nx), jnp.bfloat16),
            pltpu.VMEM((inlets, plates, nx), f32),
            pltpu.VMEM((2, 8, nx), f32),
            pltpu.SMEM(plate_order.shape, i32),
            pltpu.SMEM((per,), f32),
            pltpu.SMEM((per,), f32),
            pltpu.VMEM((2, 8, nx), f32),
            pltpu.VMEM((2, count, 8, nx), f32),
            pltpu.VMEM((2, rows2, nx), f32),
            pltpu.VMEM((2, count, rows2, nx), f32),
            dma((8,)), dma((8,)), dma((8,)), dma((8,)),
            dma((2,)), dma((2,)), dma((2,)), dma((2,)), dma((6,)),
        ],
        compiler_params=pltpu.CompilerParams(
            collective_id=0, has_side_effects=True, vmem_limit_bytes=60 * 1024 * 1024
        ),
    )(right_side, diagonal, inlet_index, plate_order, conductance, plate_level)
    sol, res, flow = pl.pallas_call(
        deliver,
        out_shape=shapes,
        in_specs=[VMEM] * 3,
        out_specs=(ANY,) * 3,
        scratch_shapes=[dma((3,))],
        compiler_params=pltpu.CompilerParams(vmem_limit_bytes=1024 * 1024),
    )(*results)
    return sol, res, flow.reshape(per)


def solution(mesh):
    in_specs = (
        P("slab", "tile", None),
        P("slab", "tile", None),
        P("slab", "tile", None, None),
        P(),
        P("tile"),
        P("tile"),
    )
    out_specs = (P("slab", "tile", None), P("slab", "tile", None), P("tile"))
    return jax.shard_map(
        functools.partial(on_device, mesh.shape["slab"], mesh.shape["tile"]),
        mesh=mesh, in_specs=in_specs, out_specs=out_specs, check_vma=False,
    )
```

```python
import functools

import jax
import jax.numpy as jnp
from jax import lax
from jax.experimental import pallas as pl
from jax.experimental.pallas import tpu as pltpu
from jax.sharding import PartitionSpec as P

STEPS = 4
HALO = 4
PAD = 8
MESH = pl.DeviceIdType.MESH
PAIRS = [(i, j) for i in range(5) for j in range(i, 5)]
ANY = pl.BlockSpec(memory_space=pl.ANY)
VMEM = pl.BlockSpec(memory_space=pltpu.VMEM)
DIRS = [(dz, dy) for dz in (-1, 0, 1) for dy in (-1, 0, 1) if (dz, dy) != (0, 0)]


def solve4(m, g):
    m = [list(row) for row in m]
    g = list(g)
    inv = [None] * 4
    for k in range(4):
        inv[k] = 1.0 / m[k][k]
        for i in range(k + 1, 4):
            fac = m[i][k] * inv[k]
            for j in range(k + 1, i + 1):
                m[i][j] = m[i][j] - fac * m[j][k]
            g[i] = g[i] - fac * g[k]
    c = [None] * 4
    for k in range(3, -1, -1):
        value = g[k]
        for i in range(k + 1, 4):
            value = value - m[i][k] * c[i]
        c[k] = value * inv[k]
    return c


def to_lanes(column, at):
    sub = lax.broadcasted_iota(jnp.int32, column.shape, 0)
    lane = lax.broadcasted_iota(jnp.int32, column.shape, 1)
    return jnp.sum(jnp.where(lane + at == sub, column, 0.0), axis=0, keepdims=True)


def coefficients(row):
    sub = lax.broadcasted_iota(jnp.int32, (16, row.shape[1]), 0)
    lane = lax.broadcasted_iota(jnp.int32, (16, row.shape[1]), 1)
    full = jnp.sum(jnp.where(lane == sub, row, 0.0), axis=1, keepdims=True)
    full = jnp.broadcast_to(full, sub.shape)
    gram = {}
    for at, (i, j) in enumerate(PAIRS):
        gram[i, j] = gram[j, i] = full[at : at + 1, :]
    m = [
        [
            3.5 * ((gram[i, j + 1] + gram[i, j]) + (gram[j, i + 1] + gram[j, i]))
            if j <= i
            else None
            for j in range(4)
        ]
        for i in range(4)
    ]
    return solve4(m, [gram[i, 0] for i in range(4)])


def kernel(
    n_slab, n_tile, rs, diag, index, order_in, conduct_in, level_in,
    sol, res, flow,
    ext, basis, dm, wt, cells, first, here, coeffs,
    order, conduct, level, msg1, part1, msg2, part2,
    h1s, h1r, h2s, h2r, a1s, a1r, a2s, a2r, local,
):
    cz, cy, nx = rs.shape
    inlets, plates = index.shape[2], index.shape[3]
    per = conduct.shape[0]
    me_s, me_t = lax.axis_index("slab"), lax.axis_index("tile")
    count, me = n_slab * n_tile, me_s * n_tile + me_t
    z_all, y_all = cz + 2 * HALO, cy + 2 * PAD
    own_z, own_y = slice(HALO, HALO + cz), slice(PAD, PAD + cy)

    def halo_cut(at):
        dz, dy = DIRS[at]
        wide = HALO - 1 if dz and dy else HALO
        src_z = {-1: slice(HALO, HALO + wide), 0: own_z, 1: slice(HALO + cz - wide, HALO + cz)}[dz]
        dst_z = {-1: slice(HALO + cz, HALO + cz + wide), 0: own_z, 1: slice(HALO - wide, HALO)}[dz]
        src_y = {-1: slice(PAD, PAD + wide), 0: own_y, 1: slice(PAD + cy - wide, PAD + cy)}[dy]
        dst_y = {-1: slice(PAD + cy, PAD + cy + wide), 0: own_y, 1: slice(PAD - wide, PAD)}[dy]
        return (src_z, src_y), (dst_z, dst_y)

    own = lambda lead: ext.at[lead, pl.ds(HALO, cz), pl.ds(PAD, cy)]
    loads = [
        pltpu.make_async_copy(src, dst, local.at[at])
        for at, (src, dst) in enumerate([
            (rs, own(0)), (diag, own(1)), (index.at[0, 0], cells),
            (order_in, order), (conduct_in, conduct), (level_in, level),
        ])
    ]
    for load in loads:
        load.start()

    barrier = pltpu.get_barrier_semaphore()

    def there(dz, dy):
        s, t = me_s + dz, me_t + dy
        return s, t, (s >= 0) & (s < n_slab) & (t >= 0) & (t < n_tile)

    def place(i):
        at = lax.rem(me + i, count)
        return lax.div(at, n_tile), lax.rem(at, n_tile)

    def every_other(body):
        if count <= 32:
            slabs = [lax.rem(me_s + i, n_slab) for i in range(n_slab)]
            tiles = [lax.rem(me_t + i, n_tile) for i in range(n_tile)]
            for j in range(n_tile):
                for i in range(n_slab):
                    if i or j:
                        body((slabs[i], tiles[j]))
        else:
            lax.fori_loop(1, count, lambda i, c: (body(place(i)), c)[1], 0)

    every_other(lambda device: pl.semaphore_signal(
        barrier, inc=1, device_id=device, device_id_type=MESH))

    for at, (dz, dy) in enumerate(DIRS):

        @pl.when(jnp.logical_not(there(-dz, -dy)[2]))
        def _():
            z, y = halo_cut(at)[1]
            ext[:, z, y, :] = jnp.zeros((3, z.stop - z.start, y.stop - y.start, nx), jnp.float32)

    loads[0].wait()
    loads[1].wait()
    pl.semaphore_wait(barrier, count - 1)

    def halo_copy(ref, lead, at, send, recv):
        dz, dy = DIRS[at]
        src, dst = halo_cut(at)
        cut = lambda z, y: ref.at[
            lead + (pl.ds(z.start, z.stop - z.start), pl.ds(y.start, y.stop - y.start))
        ]
        return pltpu.make_async_remote_copy(
            src_ref=cut(*src), dst_ref=cut(*dst),
            send_sem=send.at[at], recv_sem=recv.at[at],
            device_id=(me_s + dz, me_t + dy), device_id_type=MESH,
        )

    def halo_start(ref, lead, send, recv):
        for at, (dz, dy) in enumerate(DIRS):

            @pl.when(there(dz, dy)[2])
            def _():
                halo_copy(ref, lead, at, send, recv).start()

    def halo_recv(ref, lead, send, recv):
        for at, (dz, dy) in enumerate(DIRS):

            @pl.when(there(-dz, -dy)[2])
            def _():
                halo_copy(ref, lead, at, send, recv).wait_recv()

    def halo_sent(ref, lead, send, recv):
        for at, (dz, dy) in enumerate(DIRS):

            @pl.when(there(dz, dy)[2])
            def _():
                halo_copy(ref, lead, at, send, recv).wait_send()

    halo_start(ext, (pl.ds(0, 2),), h1s, h1r)

    loads[2].wait()
    lanes = lax.broadcasted_iota(jnp.int32, (plates, nx), 1)
    padded = jnp.concatenate(
        [cells[...], jnp.zeros((nx - inlets, plates), jnp.int32)], axis=0
    )
    if plates % nx:
        padded = jnp.concatenate(
            [padded, jnp.zeros((nx, nx - plates % nx), jnp.int32)], axis=1
        )
    spots = jnp.concatenate(
        [padded[:, at : at + nx].T for at in range(0, padded.shape[1], nx)], axis=0
    )[:plates]
    spot_line = lax.div(spots, jnp.full_like(spots, nx))
    spot_lane = spots - spot_line * nx
    for slot in range(inlets):
        line = jnp.broadcast_to(spot_line[:, slot : slot + 1], (plates, nx)) == lanes
        line = jnp.where(line, 1.0, 0.0).astype(jnp.bfloat16)
        first[slot] = jnp.concatenate([line, line], axis=1)
        lane = jnp.broadcast_to(spot_lane[:, slot : slot + 1], (plates, nx)) == lanes
        here[slot] = jnp.where(lane, 1.0, 0.0)

    for z in range(z_all):
        gz = me_s * cz + (z - HALO)
        gy = me_t * cy - PAD + lax.broadcasted_iota(jnp.int32, (y_all, nx), 0)
        inside = (gy >= 0) & (gy < n_tile * cy) & (gz >= 0) & (gz < n_slab * cz)
        wt[z] = jnp.where(inside, 1.0 / 7.0, 0.0)

    halo_recv(ext, (pl.ds(0, 2),), h1s, h1r)
    for z in range(z_all):
        dm[z] = (ext[1, z] - 1.0) * (1.0 / 7.0)

    lane_at = lax.broadcasted_iota(jnp.int32, (y_all, nx), 1)

    def powers(read, store):
        for k in range(STEPS):
            for z in range(k + 1, z_all - 1 - k):
                c = read(k, z)
                beside = read(k, z + 1) + read(k, z - 1)
                beside = beside + (pltpu.roll(c, 1, 0) + pltpu.roll(c, y_all - 1, 0))
                beside = beside + (
                    jnp.where(lane_at == 0, 0.0, pltpu.roll(c, 1, 1))
                    + jnp.where(lane_at == nx - 1, 0.0, pltpu.roll(c, nx - 1, 1))
                )
                made = dm[z] * c - wt[z] * beside
                if k == STEPS - 1:
                    store[k, z, own_y, :] = made[own_y]
                else:
                    store[k, z] = made

    def products(own):
        acc = [None] * len(PAIRS)
        for z in range(HALO, HALO + cz):
            v = [own(k, z) for k in range(5)]
            for at, (i, j) in enumerate(PAIRS):
                term = v[i] * v[j]
                acc[at] = term if acc[at] is None else acc[at] + term
        rows = [jnp.sum(term, axis=0, keepdims=True) for term in acc]
        rows = jnp.concatenate(rows + [jnp.zeros((1, nx), jnp.float32)], axis=0)
        column = jnp.broadcast_to(jnp.sum(rows, axis=1, keepdims=True), rows.shape)
        return to_lanes(column, 0)

    def inlet_sums(fields):
        halves = []
        for field in fields:
            high = field.astype(jnp.bfloat16)
            low = (field - high.astype(jnp.float32)).astype(jnp.bfloat16)
            halves.append(jnp.concatenate([high, low], axis=0))
        got = jnp.dot(
            first[...].reshape(inlets * plates, 2 * nx),
            jnp.concatenate(halves, axis=1),
            preferred_element_type=jnp.float32,
        )
        sums = []
        for at in range(len(fields)):
            total = None
            for slot in range(inlets):
                term = here[slot] * got[
                    slot * plates : (slot + 1) * plates, at * nx : (at + 1) * nx
                ]
                total = term if total is None else total + term
            total = jnp.sum(total, axis=1, keepdims=True)
            sums.append(jnp.broadcast_to(total, (plates, nx)))
        return sums

    def send(msg, slots, at, rows, send_sem, recv_sem):
        send_sem, recv_sem = send_sem.at[at.start], recv_sem.at[at.start]

        def copy(device):
            return pltpu.make_async_remote_copy(
                src_ref=msg.at[at, pl.ds(0, rows)], dst_ref=slots.at[me, at, pl.ds(0, rows)],
                send_sem=send_sem, recv_sem=recv_sem,
                device_id=device, device_id_type=MESH,
            )

        others = slots.at[pl.ds(0, count - 1), at, pl.ds(0, rows)]
        every = pltpu.make_async_remote_copy(
            src_ref=others, dst_ref=others, send_sem=send_sem, recv_sem=recv_sem,
            device_id=place(1), device_id_type=MESH,
        )
        def start():
            every_other(lambda device: copy(device).start())
            slots[me, at, 0:rows, :] = msg[at, 0:rows, :]

        def total():
            every.wait_recv()
            if count <= 32:
                parts = [slots[i, at, 0:rows, :] for i in range(count)]
                while len(parts) > 1:
                    parts = [
                        parts[i] + parts[i + 1] if i + 1 < len(parts) else parts[i]
                        for i in range(0, len(parts), 2)
                    ]
                return parts[0]
            return lax.fori_loop(
                1, count, lambda i, t: t + slots[i, at, 0:rows, :], slots[0, at, 0:rows, :]
            )

        return start, total, every.wait_send

    blocks = -(-plates // nx)
    grams = lambda at: send(msg1, part1, pl.ds(at, 1), 1, a1s, a1r)
    start2, total2, sent2 = send(msg2, part2, pl.ds(0, 2), 4 * blocks, a2s, a2r)
    sol[...] = jnp.zeros_like(sol)

    def one_block(repeat, carry):
        v0 = 2 * repeat

        def read(k, z):
            return ext[v0, z] if k == 0 else basis[k - 1, z]

        def own(k, z):
            return ext[v0, z, own_y, :] if k == 0 else basis[k - 1, z, own_y, :]

        powers(read, basis)
        msg1[repeat, 0:1, :] = products(own)
        start, total, _ = grams(repeat)
        start()

        picked = inlet_sums([
            jnp.concatenate([own(k, z) for z in range(HALO, HALO + cz)], axis=0)
            for k in range(4)
        ])
        for k, column in enumerate(picked):
            for at in range(blocks):
                row = k * blocks + at
                msg2[repeat, row : row + 1, :] = to_lanes(column, at * nx)

        @pl.when(repeat == 1)
        def _():
            start2()

        c = coefficients(total()[0])
        for k in range(4):
            coeffs[repeat, k : k + 1, :] = c[k]
        for z in range(HALO, HALO + cz):
            v = [own(k, z) for k in range(5)]
            x = sol[z - HALO]
            r = v[0]
            for k in range(4):
                x = x + c[k] * v[k]
                r = r - (7.0 * c[k]) * (v[k + 1] + v[k])
            sol[z - HALO] = x
            res[z - HALO] = r

        @pl.when(repeat == 0)
        def _():
            ext[2, own_z, own_y, :] = res[...]
            halo_start(ext, (2,), h2s, h2r)
            halo_recv(ext, (2,), h2s, h2r)

        return carry

    lax.fori_loop(0, 2, one_block, 0)

    lane1 = lax.broadcasted_iota(jnp.int32, (1, nx), 1)
    scale = 1.0 / (float(count * inlets) ** 0.5)
    contrib = [0.0] * blocks
    inlet_total = total2()
    for repeat in range(2):
        sums = inlet_total[repeat]
        for k in range(4):
            for at in range(blocks):
                row = k * blocks + at
                contrib[at] = (
                    contrib[at] + coeffs[repeat, k : k + 1, :] * sums[row : row + 1, :]
                )
    for load in loads[3:]:
        load.wait()
    row = jnp.zeros((1, nx), jnp.float32)
    for j in range(per):
        plate = order[me_t * per + j]
        header = jnp.zeros((1, nx), jnp.float32)
        for at in range(blocks):
            header = header + jnp.where(lane1 + at * nx == plate, contrib[at], 0.0)
        header = jnp.sum(header, axis=1, keepdims=True)
        row = jnp.where(lane1 == j, conduct[j] * (header * scale - level[j]), row)
    flow[...] = row[:, :per]

    for repeat in range(2):
        grams(repeat)[2]()
    sent2()
    halo_sent(ext, (pl.ds(0, 2),), h1s, h1r)
    halo_sent(ext, (2,), h2s, h2r)


def deliver(sol, res, flow, sol_out, res_out, flow_out, sems):
    copies = [
        pltpu.make_async_copy(src, dst, sems.at[at])
        for at, (src, dst) in enumerate([(sol, sol_out), (res, res_out), (flow, flow_out)])
    ]
    for copy in copies:
        copy.start()
    for copy in copies:
        copy.wait()


def on_device(n_slab, n_tile, right_side, diagonal, inlet_index, plate_order, conductance, plate_level):
    cz, cy, nx = right_side.shape
    inlet_index = inlet_index.transpose(0, 1, 3, 2)
    inlets, plates = inlet_index.shape[2:]
    per = conductance.shape[0]
    z_all, y_all = cz + 2 * HALO, cy + 2 * PAD
    count = n_slab * n_tile
    rows2 = 8 * -(-4 * -(-plates // nx) // 8)
    f32, i32 = jnp.float32, jnp.int32
    block = jax.ShapeDtypeStruct((cz, cy, nx), f32)
    shapes = (block, block, jax.ShapeDtypeStruct((1, per), f32))
    dma = pltpu.SemaphoreType.DMA
    results = pl.pallas_call(
        functools.partial(kernel, n_slab, n_tile),
        out_shape=tuple(pltpu.VMEM(leaf.shape, leaf.dtype) for leaf in shapes),
        in_specs=[ANY] * 6,
        out_specs=(VMEM,) * 3,
        scratch_shapes=[
            pltpu.VMEM((3, z_all, y_all, nx), f32),
            pltpu.VMEM((4, z_all, y_all, nx), f32),
            pltpu.VMEM((z_all, y_all, nx), f32),
            pltpu.VMEM((z_all, y_all, nx), f32),
            pltpu.VMEM((inlets, plates), i32),
            pltpu.VMEM((inlets, plates, 2 * nx), jnp.bfloat16),
            pltpu.VMEM((inlets, plates, nx), f32),
            pltpu.VMEM((2, 8, nx), f32),
            pltpu.SMEM(plate_order.shape, i32),
            pltpu.SMEM((per,), f32),
            pltpu.SMEM((per,), f32),
            pltpu.VMEM((2, 8, nx), f32),
            pltpu.VMEM((count, 2, 8, nx), f32),
            pltpu.VMEM((2, rows2, nx), f32),
            pltpu.VMEM((count, 2, rows2, nx), f32),
            dma((8,)), dma((8,)), dma((8,)), dma((8,)),
            dma((2,)), dma((2,)), dma((2,)), dma((2,)), dma((6,)),
        ],
        compiler_params=pltpu.CompilerParams(
            collective_id=0, has_side_effects=True, vmem_limit_bytes=60 * 1024 * 1024
        ),
    )(right_side, diagonal, inlet_index, plate_order, conductance, plate_level)
    sol, res, flow = pl.pallas_call(
        deliver,
        out_shape=shapes,
        in_specs=[VMEM] * 3,
        out_specs=(ANY,) * 3,
        scratch_shapes=[dma((3,))],
        compiler_params=pltpu.CompilerParams(vmem_limit_bytes=1024 * 1024),
    )(*results)
    return sol, res, flow.reshape(per)


def solution(mesh):
    in_specs = (
        P("slab", "tile", None),
        P("slab", "tile", None),
        P("slab", "tile", None, None),
        P(),
        P("tile"),
        P("tile"),
    )
    out_specs = (P("slab", "tile", None), P("slab", "tile", None), P("tile"))
    return jax.shard_map(
        functools.partial(on_device, mesh.shape["slab"], mesh.shape["tile"]),
        mesh=mesh, in_specs=in_specs, out_specs=out_specs, check_vma=False,
    )
```

```python
import functools

import jax
import jax.numpy as jnp
from jax import lax
from jax.experimental import pallas as pl
from jax.experimental.pallas import tpu as pltpu
from jax.sharding import PartitionSpec as P

STEPS = 4
HALO = 4
PAD = 8
MESH = pl.DeviceIdType.MESH
PAIRS = [(i, j) for i in range(5) for j in range(i, 5)]
ANY = pl.BlockSpec(memory_space=pl.ANY)
VMEM = pl.BlockSpec(memory_space=pltpu.VMEM)
DIRS = [(dz, dy) for dz in (-1, 0, 1) for dy in (-1, 0, 1) if (dz, dy) != (0, 0)]


def solve4(m, g):
    m = [list(row) for row in m]
    g = list(g)
    inv = [None] * 4
    for k in range(4):
        inv[k] = 1.0 / m[k][k]
        for i in range(k + 1, 4):
            fac = m[i][k] * inv[k]
            for j in range(k + 1, i + 1):
                m[i][j] = m[i][j] - fac * m[j][k]
            g[i] = g[i] - fac * g[k]
    c = [None] * 4
    for k in range(3, -1, -1):
        value = g[k]
        for i in range(k + 1, 4):
            value = value - m[i][k] * c[i]
        c[k] = value * inv[k]
    return c


def to_lanes(columns, at):
    rows = columns[0].shape[0]
    sub = lax.broadcasted_iota(jnp.int32, columns[0].shape, 0)
    lane = lax.broadcasted_iota(jnp.int32, columns[0].shape, 1)
    total = None
    for k, column in enumerate(columns):
        term = jnp.where(lane + (at - k * rows) == sub, column, 0.0)
        total = term if total is None else total + term
    return jnp.sum(total, axis=0, keepdims=True)


def coefficients(row):
    sub = lax.broadcasted_iota(jnp.int32, (16, row.shape[1]), 0)
    lane = lax.broadcasted_iota(jnp.int32, (16, row.shape[1]), 1)
    full = jnp.sum(jnp.where(lane == sub, row, 0.0), axis=1, keepdims=True)
    full = jnp.broadcast_to(full, sub.shape)
    gram = {}
    for at, (i, j) in enumerate(PAIRS):
        gram[i, j] = gram[j, i] = full[at : at + 1, :]
    m = [
        [
            3.5 * ((gram[i, j + 1] + gram[i, j]) + (gram[j, i + 1] + gram[j, i]))
            if j <= i
            else None
            for j in range(4)
        ]
        for i in range(4)
    ]
    return solve4(m, [gram[i, 0] for i in range(4)])


def kernel(
    n_slab, n_tile, rs, diag, index, order_in, conduct_in, level_in,
    sol, res, flow,
    ext, basis, dm, wt, cells, first, here, coeffs,
    order, conduct, level, msg1, part1, msg2, part2,
    h1s, h1r, h2s, h2r, a1s, a1r, a2s, a2r, local,
):
    cz, cy, nx = rs.shape
    inlets, plates = index.shape[2], index.shape[3]
    per = conduct.shape[0]
    me_s, me_t = lax.axis_index("slab"), lax.axis_index("tile")
    count, me = n_slab * n_tile, me_s * n_tile + me_t
    z_all, y_all = cz + 2 * HALO, cy + 2 * PAD
    own_z, own_y = slice(HALO, HALO + cz), slice(PAD, PAD + cy)

    def halo_cut(at):
        dz, dy = DIRS[at]
        wide = HALO - 1 if dz and dy else HALO
        src_z = {-1: slice(HALO, HALO + wide), 0: own_z, 1: slice(HALO + cz - wide, HALO + cz)}[dz]
        dst_z = {-1: slice(HALO + cz, HALO + cz + wide), 0: own_z, 1: slice(HALO - wide, HALO)}[dz]
        src_y = {-1: slice(PAD, PAD + wide), 0: own_y, 1: slice(PAD + cy - wide, PAD + cy)}[dy]
        dst_y = {-1: slice(PAD + cy, PAD + cy + wide), 0: own_y, 1: slice(PAD - wide, PAD)}[dy]
        return (src_z, src_y), (dst_z, dst_y)

    own = lambda lead: ext.at[lead, pl.ds(HALO, cz), pl.ds(PAD, cy)]
    loads = [
        pltpu.make_async_copy(src, dst, local.at[at])
        for at, (src, dst) in enumerate([
            (rs, own(0)), (diag, own(1)), (index.at[0, 0], cells),
            (order_in, order), (conduct_in, conduct), (level_in, level),
        ])
    ]
    for load in loads:
        load.start()

    barrier = pltpu.get_barrier_semaphore()

    def there(dz, dy):
        s, t = me_s + dz, me_t + dy
        return s, t, (s >= 0) & (s < n_slab) & (t >= 0) & (t < n_tile)

    def place(i):
        at = lax.rem(me + i, count)
        return lax.div(at, n_tile), lax.rem(at, n_tile)

    def every_other(body):
        if count <= 32:
            slabs = [lax.rem(me_s + i, n_slab) for i in range(n_slab)]
            tiles = [lax.rem(me_t + i, n_tile) for i in range(n_tile)]
            for j in range(n_tile):
                for i in range(n_slab):
                    if i or j:
                        body((slabs[i], tiles[j]))
        else:
            lax.fori_loop(1, count, lambda i, c: (body(place(i)), c)[1], 0)

    every_other(lambda device: pl.semaphore_signal(
        barrier, inc=1, device_id=device, device_id_type=MESH))

    for at, (dz, dy) in enumerate(DIRS):

        @pl.when(jnp.logical_not(there(-dz, -dy)[2]))
        def _():
            z, y = halo_cut(at)[1]
            ext[:, z, y, :] = jnp.zeros((3, z.stop - z.start, y.stop - y.start, nx), jnp.float32)

    loads[0].wait()
    loads[1].wait()
    pl.semaphore_wait(barrier, count - 1)

    def halo_copy(ref, lead, at, send, recv):
        dz, dy = DIRS[at]
        src, dst = halo_cut(at)
        cut = lambda z, y: ref.at[
            lead + (pl.ds(z.start, z.stop - z.start), pl.ds(y.start, y.stop - y.start))
        ]
        return pltpu.make_async_remote_copy(
            src_ref=cut(*src), dst_ref=cut(*dst),
            send_sem=send.at[at], recv_sem=recv.at[at],
            device_id=(me_s + dz, me_t + dy), device_id_type=MESH,
        )

    def halo_start(ref, lead, send, recv):
        for at, (dz, dy) in enumerate(DIRS):

            @pl.when(there(dz, dy)[2])
            def _():
                halo_copy(ref, lead, at, send, recv).start()

    def halo_recv(ref, lead, send, recv):
        for at, (dz, dy) in enumerate(DIRS):

            @pl.when(there(-dz, -dy)[2])
            def _():
                halo_copy(ref, lead, at, send, recv).wait_recv()

    def halo_sent(ref, lead, send, recv):
        for at, (dz, dy) in enumerate(DIRS):

            @pl.when(there(dz, dy)[2])
            def _():
                halo_copy(ref, lead, at, send, recv).wait_send()

    halo_start(ext, (pl.ds(0, 2),), h1s, h1r)

    loads[2].wait()
    lanes = lax.broadcasted_iota(jnp.int32, (plates, nx), 1)
    padded = jnp.concatenate(
        [cells[...], jnp.zeros((nx - inlets, plates), jnp.int32)], axis=0
    )
    if plates % nx:
        padded = jnp.concatenate(
            [padded, jnp.zeros((nx, nx - plates % nx), jnp.int32)], axis=1
        )
    spots = jnp.concatenate(
        [padded[:, at : at + nx].T for at in range(0, padded.shape[1], nx)], axis=0
    )[:plates]
    spot_line = lax.div(spots, jnp.full_like(spots, nx))
    spot_lane = spots - spot_line * nx
    for slot in range(inlets):
        line = jnp.broadcast_to(spot_line[:, slot : slot + 1], (plates, nx)) == lanes
        line = jnp.where(line, 1.0, 0.0).astype(jnp.bfloat16)
        first[slot] = jnp.concatenate([line, line], axis=1)
        lane = jnp.broadcast_to(spot_lane[:, slot : slot + 1], (plates, nx)) == lanes
        here[slot] = jnp.where(lane, 1.0, 0.0)

    for z in range(z_all):
        gz = me_s * cz + (z - HALO)
        gy = me_t * cy - PAD + lax.broadcasted_iota(jnp.int32, (y_all, nx), 0)
        inside = (gy >= 0) & (gy < n_tile * cy) & (gz >= 0) & (gz < n_slab * cz)
        wt[z] = jnp.where(inside, 1.0 / 7.0, 0.0)

    halo_recv(ext, (pl.ds(0, 2),), h1s, h1r)
    for z in range(z_all):
        dm[z] = (ext[1, z] - 1.0) * (1.0 / 7.0)

    lane_at = lax.broadcasted_iota(jnp.int32, (y_all, nx), 1)

    def powers(read, store):
        for k in range(STEPS):
            for z in range(k + 1, z_all - 1 - k):
                c = read(k, z)
                beside = read(k, z + 1) + read(k, z - 1)
                beside = beside + (pltpu.roll(c, 1, 0) + pltpu.roll(c, y_all - 1, 0))
                beside = beside + (
                    jnp.where(lane_at == 0, 0.0, pltpu.roll(c, 1, 1))
                    + jnp.where(lane_at == nx - 1, 0.0, pltpu.roll(c, nx - 1, 1))
                )
                made = dm[z] * c - wt[z] * beside
                if k == STEPS - 1:
                    store[k, z, own_y, :] = made[own_y]
                else:
                    store[k, z] = made

    def products(own):
        acc = [None] * len(PAIRS)
        for z in range(HALO, HALO + cz):
            v = [own(k, z) for k in range(5)]
            for at, (i, j) in enumerate(PAIRS):
                term = v[i] * v[j]
                acc[at] = term if acc[at] is None else acc[at] + term
        rows = [jnp.sum(term, axis=0, keepdims=True) for term in acc]
        rows = jnp.concatenate(rows + [jnp.zeros((1, nx), jnp.float32)], axis=0)
        column = jnp.broadcast_to(jnp.sum(rows, axis=1, keepdims=True), rows.shape)
        return to_lanes([column], 0)

    def inlet_sums(fields):
        halves = []
        for field in fields:
            high = field.astype(jnp.bfloat16)
            low = (field - high.astype(jnp.float32)).astype(jnp.bfloat16)
            halves.append(jnp.concatenate([high, low], axis=0))
        got = jnp.dot(
            first[...].reshape(inlets * plates, 2 * nx),
            jnp.concatenate(halves, axis=1),
            preferred_element_type=jnp.float32,
        )
        sums = []
        for at in range(len(fields)):
            total = None
            for slot in range(inlets):
                term = here[slot] * got[
                    slot * plates : (slot + 1) * plates, at * nx : (at + 1) * nx
                ]
                total = term if total is None else total + term
            total = jnp.sum(total, axis=1, keepdims=True)
            sums.append(jnp.broadcast_to(total, (plates, nx)))
        return sums

    def send(msg, slots, at, rows, send_sem, recv_sem):
        send_sem, recv_sem = send_sem.at[at], recv_sem.at[at]

        def copy(device):
            return pltpu.make_async_remote_copy(
                src_ref=msg.at[at, pl.ds(0, rows)], dst_ref=slots.at[at, me, pl.ds(0, rows)],
                send_sem=send_sem, recv_sem=recv_sem,
                device_id=device, device_id_type=MESH,
            )

        others = slots.at[at, pl.ds(0, count - 1), pl.ds(0, rows)]
        every = pltpu.make_async_remote_copy(
            src_ref=others, dst_ref=others, send_sem=send_sem, recv_sem=recv_sem,
            device_id=place(1), device_id_type=MESH,
        )
        def start():
            every_other(lambda device: copy(device).start())
            slots[at, me, 0:rows, :] = msg[at, 0:rows, :]

        def total():
            every.wait_recv()
            if count <= 32:
                parts = [slots[at, i, 0:rows, :] for i in range(count)]
                while len(parts) > 1:
                    parts = [
                        parts[i] + parts[i + 1] if i + 1 < len(parts) else parts[i]
                        for i in range(0, len(parts), 2)
                    ]
                return parts[0]
            return lax.fori_loop(
                1, count, lambda i, t: t + slots[at, i, 0:rows, :], slots[at, 0, 0:rows, :]
            )

        return start, total, every.wait_send

    blocks = -(-4 * plates // nx)
    grams = lambda at: send(msg1, part1, at, 1, a1s, a1r)
    inlet = lambda at: send(msg2, part2, at, blocks, a2s, a2r)
    sol[...] = jnp.zeros_like(sol)

    def one_block(repeat, carry):
        v0 = 2 * repeat

        def read(k, z):
            return ext[v0, z] if k == 0 else basis[k - 1, z]

        def own(k, z):
            return ext[v0, z, own_y, :] if k == 0 else basis[k - 1, z, own_y, :]

        powers(read, basis)
        msg1[repeat, 0:1, :] = products(own)
        start, total, _ = grams(repeat)
        start()

        picked = inlet_sums([
            jnp.concatenate([own(k, z) for z in range(HALO, HALO + cz)], axis=0)
            for k in range(4)
        ])
        for at in range(blocks):
            msg2[repeat, at : at + 1, :] = to_lanes(picked, at * nx)
        inlet(repeat)[0]()

        c = coefficients(total())
        for k in range(4):
            coeffs[repeat, k : k + 1, :] = c[k]
        for z in range(HALO, HALO + cz):
            v = [own(k, z) for k in range(5)]
            x = sol[z - HALO]
            r = v[0]
            for k in range(4):
                x = x + c[k] * v[k]
                r = r - (7.0 * c[k]) * (v[k + 1] + v[k])
            sol[z - HALO] = x
            res[z - HALO] = r

        @pl.when(repeat == 0)
        def _():
            ext[2, own_z, own_y, :] = res[...]
            halo_start(ext, (2,), h2s, h2r)
            halo_recv(ext, (2,), h2s, h2r)

        return carry

    lax.fori_loop(0, 2, one_block, 0)

    lane1 = lax.broadcasted_iota(jnp.int32, (1, nx), 1)
    scale = 1.0 / (float(count * inlets) ** 0.5)
    contrib = [0.0] * blocks
    for repeat in range(2):
        sums = inlet(repeat)[1]()
        for at in range(blocks):
            spot = lane1 + at * nx
            weight = coeffs[repeat, 3:4, :]
            for k in (2, 1, 0):
                weight = jnp.where(spot < (k + 1) * plates, coeffs[repeat, k : k + 1, :], weight)
            weight = jnp.where(spot < 4 * plates, weight, 0.0)
            contrib[at] = contrib[at] + weight * sums[at : at + 1, :]
    for load in loads[3:]:
        load.wait()
    row = jnp.zeros((1, nx), jnp.float32)
    for j in range(per):
        plate = order[me_t * per + j]
        header = jnp.zeros((1, nx), jnp.float32)
        for at in range(blocks):
            for k in range(4):
                mine = lane1 + at * nx == plate + k * plates
                header = header + jnp.where(mine, contrib[at], 0.0)
        header = jnp.sum(header, axis=1, keepdims=True)
        row = jnp.where(lane1 == j, conduct[j] * (header * scale - level[j]), row)
    flow[...] = row[:, :per]

    for repeat in range(2):
        grams(repeat)[2]()
        inlet(repeat)[2]()
    halo_sent(ext, (pl.ds(0, 2),), h1s, h1r)
    halo_sent(ext, (2,), h2s, h2r)


def deliver(sol, res, flow, sol_out, res_out, flow_out, sems):
    copies = [
        pltpu.make_async_copy(src, dst, sems.at[at])
        for at, (src, dst) in enumerate([(sol, sol_out), (res, res_out), (flow, flow_out)])
    ]
    for copy in copies:
        copy.start()
    for copy in copies:
        copy.wait()


def on_device(n_slab, n_tile, right_side, diagonal, inlet_index, plate_order, conductance, plate_level):
    cz, cy, nx = right_side.shape
    inlet_index = inlet_index.transpose(0, 1, 3, 2)
    inlets, plates = inlet_index.shape[2:]
    per = conductance.shape[0]
    z_all, y_all = cz + 2 * HALO, cy + 2 * PAD
    count = n_slab * n_tile
    rows2 = 8 * -(-4 * plates // (8 * nx))
    f32, i32 = jnp.float32, jnp.int32
    block = jax.ShapeDtypeStruct((cz, cy, nx), f32)
    shapes = (block, block, jax.ShapeDtypeStruct((1, per), f32))
    dma = pltpu.SemaphoreType.DMA
    results = pl.pallas_call(
        functools.partial(kernel, n_slab, n_tile),
        out_shape=tuple(pltpu.VMEM(leaf.shape, leaf.dtype) for leaf in shapes),
        in_specs=[ANY] * 6,
        out_specs=(VMEM,) * 3,
        scratch_shapes=[
            pltpu.VMEM((3, z_all, y_all, nx), f32),
            pltpu.VMEM((4, z_all, y_all, nx), f32),
            pltpu.VMEM((z_all, y_all, nx), f32),
            pltpu.VMEM((z_all, y_all, nx), f32),
            pltpu.VMEM((inlets, plates), i32),
            pltpu.VMEM((inlets, plates, 2 * nx), jnp.bfloat16),
            pltpu.VMEM((inlets, plates, nx), f32),
            pltpu.VMEM((2, 8, nx), f32),
            pltpu.SMEM(plate_order.shape, i32),
            pltpu.SMEM((per,), f32),
            pltpu.SMEM((per,), f32),
            pltpu.VMEM((2, 8, nx), f32),
            pltpu.VMEM((2, count, 8, nx), f32),
            pltpu.VMEM((2, rows2, nx), f32),
            pltpu.VMEM((2, count, rows2, nx), f32),
            dma((8,)), dma((8,)), dma((8,)), dma((8,)),
            dma((2,)), dma((2,)), dma((2,)), dma((2,)), dma((6,)),
        ],
        compiler_params=pltpu.CompilerParams(
            collective_id=0, has_side_effects=True, vmem_limit_bytes=60 * 1024 * 1024
        ),
    )(right_side, diagonal, inlet_index, plate_order, conductance, plate_level)
    sol, res, flow = pl.pallas_call(
        deliver,
        out_shape=shapes,
        in_specs=[VMEM] * 3,
        out_specs=(ANY,) * 3,
        scratch_shapes=[dma((3,))],
        compiler_params=pltpu.CompilerParams(vmem_limit_bytes=1024 * 1024),
    )(*results)
    return sol, res, flow.reshape(per)


def solution(mesh):
    in_specs = (
        P("slab", "tile", None),
        P("slab", "tile", None),
        P("slab", "tile", None, None),
        P(),
        P("tile"),
        P("tile"),
    )
    out_specs = (P("slab", "tile", None), P("slab", "tile", None), P("tile"))
    return jax.shard_map(
        functools.partial(on_device, mesh.shape["slab"], mesh.shape["tile"]),
        mesh=mesh, in_specs=in_specs, out_specs=out_specs, check_vma=False,
    )
```

```python
import functools

import jax
import jax.numpy as jnp
from jax import lax
from jax.experimental import pallas as pl
from jax.experimental.pallas import tpu as pltpu
from jax.sharding import PartitionSpec as P

STEPS = 4
HALO = 4
PAD = 8
MESH = pl.DeviceIdType.MESH
PAIRS = [(i, j) for i in range(5) for j in range(i, 5)]
ANY = pl.BlockSpec(memory_space=pl.ANY)
VMEM = pl.BlockSpec(memory_space=pltpu.VMEM)
DIRS = [(dz, dy) for dz in (-1, 0, 1) for dy in (-1, 0, 1) if (dz, dy) != (0, 0)]


def solve4(m, g):
    m = [list(row) for row in m]
    g = list(g)
    inv = [None] * 4
    for k in range(4):
        inv[k] = 1.0 / m[k][k]
        for i in range(k + 1, 4):
            fac = m[i][k] * inv[k]
            for j in range(k + 1, i + 1):
                m[i][j] = m[i][j] - fac * m[j][k]
            g[i] = g[i] - fac * g[k]
    c = [None] * 4
    for k in range(3, -1, -1):
        value = g[k]
        for i in range(k + 1, 4):
            value = value - m[i][k] * c[i]
        c[k] = value * inv[k]
    return c


def to_lanes(columns, at):
    rows = columns[0].shape[0]
    sub = lax.broadcasted_iota(jnp.int32, columns[0].shape, 0)
    lane = lax.broadcasted_iota(jnp.int32, columns[0].shape, 1)
    total = None
    for k, column in enumerate(columns):
        term = jnp.where(lane + (at - k * rows) == sub, column, 0.0)
        total = term if total is None else total + term
    return jnp.sum(total, axis=0, keepdims=True)


def coefficients(row):
    sub = lax.broadcasted_iota(jnp.int32, (16, row.shape[1]), 0)
    lane = lax.broadcasted_iota(jnp.int32, (16, row.shape[1]), 1)
    full = jnp.sum(jnp.where(lane == sub, row, 0.0), axis=1, keepdims=True)
    full = jnp.broadcast_to(full, sub.shape)
    gram = {}
    for at, (i, j) in enumerate(PAIRS):
        gram[i, j] = gram[j, i] = full[at : at + 1, :]
    m = [
        [
            3.5 * ((gram[i, j + 1] + gram[i, j]) + (gram[j, i + 1] + gram[j, i]))
            if j <= i
            else None
            for j in range(4)
        ]
        for i in range(4)
    ]
    return solve4(m, [gram[i, 0] for i in range(4)])


def kernel(
    n_slab, n_tile, rs, diag, index, order_in, conduct_in, level_in,
    sol, res, flow,
    ext, basis, dm, wt, cells, first, here, coeffs, everything,
    order, conduct, level, msg, part,
    h1s, h1r, h2s, h2r, a1s, a1r, local,
):
    cz, cy, nx = rs.shape
    inlets, plates = index.shape[2], index.shape[3]
    per = conduct.shape[0]
    me_s, me_t = lax.axis_index("slab"), lax.axis_index("tile")
    count, me = n_slab * n_tile, me_s * n_tile + me_t
    z_all, y_all = cz + 2 * HALO, cy + 2 * PAD
    own_z, own_y = slice(HALO, HALO + cz), slice(PAD, PAD + cy)

    def halo_cut(at):
        dz, dy = DIRS[at]
        wide = HALO - 1 if dz and dy else HALO
        src_z = {-1: slice(HALO, HALO + wide), 0: own_z, 1: slice(HALO + cz - wide, HALO + cz)}[dz]
        dst_z = {-1: slice(HALO + cz, HALO + cz + wide), 0: own_z, 1: slice(HALO - wide, HALO)}[dz]
        src_y = {-1: slice(PAD, PAD + wide), 0: own_y, 1: slice(PAD + cy - wide, PAD + cy)}[dy]
        dst_y = {-1: slice(PAD + cy, PAD + cy + wide), 0: own_y, 1: slice(PAD - wide, PAD)}[dy]
        return (src_z, src_y), (dst_z, dst_y)

    own = lambda lead: ext.at[lead, pl.ds(HALO, cz), pl.ds(PAD, cy)]
    loads = [
        pltpu.make_async_copy(src, dst, local.at[at])
        for at, (src, dst) in enumerate([
            (rs, own(0)), (diag, own(1)), (index.at[0, 0], cells),
            (order_in, order), (conduct_in, conduct), (level_in, level),
        ])
    ]
    for load in loads:
        load.start()

    barrier = pltpu.get_barrier_semaphore()

    def there(dz, dy):
        s, t = me_s + dz, me_t + dy
        return s, t, (s >= 0) & (s < n_slab) & (t >= 0) & (t < n_tile)

    def place(i):
        at = lax.rem(me + i, count)
        return lax.div(at, n_tile), lax.rem(at, n_tile)

    def every_other(body):
        if count <= 32:
            slabs = [lax.rem(me_s + i, n_slab) for i in range(n_slab)]
            tiles = [lax.rem(me_t + i, n_tile) for i in range(n_tile)]
            for j in range(n_tile):
                for i in range(n_slab):
                    if i or j:
                        body((slabs[i], tiles[j]))
        else:
            lax.fori_loop(1, count, lambda i, c: (body(place(i)), c)[1], 0)

    every_other(lambda device: pl.semaphore_signal(
        barrier, inc=1, device_id=device, device_id_type=MESH))

    for at, (dz, dy) in enumerate(DIRS):

        @pl.when(jnp.logical_not(there(-dz, -dy)[2]))
        def _():
            z, y = halo_cut(at)[1]
            ext[:, z, y, :] = jnp.zeros((3, z.stop - z.start, y.stop - y.start, nx), jnp.float32)

    loads[0].wait()
    loads[1].wait()
    pl.semaphore_wait(barrier, count - 1)

    def halo_copy(ref, lead, at, send, recv):
        dz, dy = DIRS[at]
        src, dst = halo_cut(at)
        cut = lambda z, y: ref.at[
            lead + (pl.ds(z.start, z.stop - z.start), pl.ds(y.start, y.stop - y.start))
        ]
        return pltpu.make_async_remote_copy(
            src_ref=cut(*src), dst_ref=cut(*dst),
            send_sem=send.at[at], recv_sem=recv.at[at],
            device_id=(me_s + dz, me_t + dy), device_id_type=MESH,
        )

    def halo_start(ref, lead, send, recv):
        for at, (dz, dy) in enumerate(DIRS):

            @pl.when(there(dz, dy)[2])
            def _():
                halo_copy(ref, lead, at, send, recv).start()

    def halo_recv(ref, lead, send, recv):
        for at, (dz, dy) in enumerate(DIRS):

            @pl.when(there(-dz, -dy)[2])
            def _():
                halo_copy(ref, lead, at, send, recv).wait_recv()

    def halo_sent(ref, lead, send, recv):
        for at, (dz, dy) in enumerate(DIRS):

            @pl.when(there(dz, dy)[2])
            def _():
                halo_copy(ref, lead, at, send, recv).wait_send()

    halo_start(ext, (pl.ds(0, 2),), h1s, h1r)

    loads[2].wait()
    lanes = lax.broadcasted_iota(jnp.int32, (plates, nx), 1)
    padded = jnp.concatenate(
        [cells[...], jnp.zeros((nx - inlets, plates), jnp.int32)], axis=0
    )
    if plates % nx:
        padded = jnp.concatenate(
            [padded, jnp.zeros((nx, nx - plates % nx), jnp.int32)], axis=1
        )
    spots = jnp.concatenate(
        [padded[:, at : at + nx].T for at in range(0, padded.shape[1], nx)], axis=0
    )[:plates]
    spot_line = lax.div(spots, jnp.full_like(spots, nx))
    spot_lane = spots - spot_line * nx
    for slot in range(inlets):
        line = jnp.broadcast_to(spot_line[:, slot : slot + 1], (plates, nx)) == lanes
        line = jnp.where(line, 1.0, 0.0).astype(jnp.bfloat16)
        first[slot] = jnp.concatenate([line, line], axis=1)
        lane = jnp.broadcast_to(spot_lane[:, slot : slot + 1], (plates, nx)) == lanes
        here[slot] = jnp.where(lane, 1.0, 0.0)

    for z in range(z_all):
        gz = me_s * cz + (z - HALO)
        gy = me_t * cy - PAD + lax.broadcasted_iota(jnp.int32, (y_all, nx), 0)
        inside = (gy >= 0) & (gy < n_tile * cy) & (gz >= 0) & (gz < n_slab * cz)
        wt[z] = jnp.where(inside, 1.0 / 7.0, 0.0)

    halo_recv(ext, (pl.ds(0, 2),), h1s, h1r)
    for z in range(z_all):
        dm[z] = (ext[1, z] - 1.0) * (1.0 / 7.0)

    lane_at = lax.broadcasted_iota(jnp.int32, (y_all, nx), 1)

    def powers(read, store):
        for k in range(STEPS):
            for z in range(k + 1, z_all - 1 - k):
                c = read(k, z)
                beside = read(k, z + 1) + read(k, z - 1)
                beside = beside + (pltpu.roll(c, 1, 0) + pltpu.roll(c, y_all - 1, 0))
                beside = beside + (
                    jnp.where(lane_at == 0, 0.0, pltpu.roll(c, 1, 1))
                    + jnp.where(lane_at == nx - 1, 0.0, pltpu.roll(c, nx - 1, 1))
                )
                made = dm[z] * c - wt[z] * beside
                if k == STEPS - 1:
                    store[k, z, own_y, :] = made[own_y]
                else:
                    store[k, z] = made

    def products(own):
        acc = [None] * len(PAIRS)
        for z in range(HALO, HALO + cz):
            v = [own(k, z) for k in range(5)]
            for at, (i, j) in enumerate(PAIRS):
                term = v[i] * v[j]
                acc[at] = term if acc[at] is None else acc[at] + term
        rows = [jnp.sum(term, axis=0, keepdims=True) for term in acc]
        rows = jnp.concatenate(rows + [jnp.zeros((1, nx), jnp.float32)], axis=0)
        column = jnp.broadcast_to(jnp.sum(rows, axis=1, keepdims=True), rows.shape)
        return to_lanes([column], 0)

    def inlet_sums(fields):
        halves = []
        for field in fields:
            high = field.astype(jnp.bfloat16)
            low = (field - high.astype(jnp.float32)).astype(jnp.bfloat16)
            halves.append(jnp.concatenate([high, low], axis=0))
        got = jnp.dot(
            first[...].reshape(inlets * plates, 2 * nx),
            jnp.concatenate(halves, axis=1),
            preferred_element_type=jnp.float32,
        )
        sums = []
        for at in range(len(fields)):
            total = None
            for slot in range(inlets):
                term = here[slot] * got[
                    slot * plates : (slot + 1) * plates, at * nx : (at + 1) * nx
                ]
                total = term if total is None else total + term
            total = jnp.sum(total, axis=1, keepdims=True)
            sums.append(jnp.broadcast_to(total, (plates, nx)))
        return sums

    def send(msg, slots, at, rows, send_sem, recv_sem):
        send_sem, recv_sem = send_sem.at[at], recv_sem.at[at]

        def copy(device):
            return pltpu.make_async_remote_copy(
                src_ref=msg.at[at, pl.ds(0, rows)], dst_ref=slots.at[at, me, pl.ds(0, rows)],
                send_sem=send_sem, recv_sem=recv_sem,
                device_id=device, device_id_type=MESH,
            )

        others = slots.at[at, pl.ds(0, count - 1), pl.ds(0, rows)]
        every = pltpu.make_async_remote_copy(
            src_ref=others, dst_ref=others, send_sem=send_sem, recv_sem=recv_sem,
            device_id=place(1), device_id_type=MESH,
        )
        def start():
            every_other(lambda device: copy(device).start())
            slots[at, me, 0:rows, :] = msg[at, 0:rows, :]

        def total():
            every.wait_recv()
            if count <= 32:
                parts = [slots[at, i, 0:rows, :] for i in range(count)]
                while len(parts) > 1:
                    parts = [
                        parts[i] + parts[i + 1] if i + 1 < len(parts) else parts[i]
                        for i in range(0, len(parts), 2)
                    ]
                return parts[0]
            return lax.fori_loop(
                1, count, lambda i, t: t + slots[at, i, 0:rows, :], slots[at, 0, 0:rows, :]
            )

        return start, total, every.wait_send

    blocks = -(-4 * plates // nx)
    rows = 1 + 2 * blocks
    sums = lambda at: send(msg, part, at, rows, a1s, a1r)
    msg[...] = jnp.zeros_like(msg)
    sol[...] = jnp.zeros_like(sol)

    def one_block(repeat, carry):
        v0 = 2 * repeat

        def read(k, z):
            return ext[v0, z] if k == 0 else basis[k - 1, z]

        def own(k, z):
            return ext[v0, z, own_y, :] if k == 0 else basis[k - 1, z, own_y, :]

        powers(read, basis)
        msg[repeat, 0:1, :] = products(own)

        def pick(first_row):
            picked = inlet_sums([
                jnp.concatenate([own(k, z) for z in range(HALO, HALO + cz)], axis=0)
                for k in range(4)
            ])
            for at in range(blocks):
                row = first_row + at
                msg[1, row : row + 1, :] = to_lanes(picked, at * nx)

        @pl.when(repeat == 1)
        def _():
            pick(1 + blocks)

        start, total, _ = sums(repeat)
        start()

        @pl.when(repeat == 0)
        def _():
            pick(1)

        everything[...] = total()
        c = coefficients(everything[0:1, :])
        for k in range(4):
            coeffs[repeat, k : k + 1, :] = c[k]
        for z in range(HALO, HALO + cz):
            v = [own(k, z) for k in range(5)]
            x = sol[z - HALO]
            r = v[0]
            for k in range(4):
                x = x + c[k] * v[k]
                r = r - (7.0 * c[k]) * (v[k + 1] + v[k])
            sol[z - HALO] = x
            res[z - HALO] = r

        @pl.when(repeat == 0)
        def _():
            ext[2, own_z, own_y, :] = res[...]
            halo_start(ext, (2,), h2s, h2r)
            halo_recv(ext, (2,), h2s, h2r)

        return carry

    lax.fori_loop(0, 2, one_block, 0)

    lane1 = lax.broadcasted_iota(jnp.int32, (1, nx), 1)
    scale = 1.0 / (float(count * inlets) ** 0.5)
    contrib = [0.0] * blocks
    for repeat in range(2):
        for at in range(blocks):
            spot = lane1 + at * nx
            weight = coeffs[repeat, 3:4, :]
            for k in (2, 1, 0):
                weight = jnp.where(spot < (k + 1) * plates, coeffs[repeat, k : k + 1, :], weight)
            weight = jnp.where(spot < 4 * plates, weight, 0.0)
            row = 1 + repeat * blocks + at
            contrib[at] = contrib[at] + weight * everything[row : row + 1, :]
    for load in loads[3:]:
        load.wait()
    row = jnp.zeros((1, nx), jnp.float32)
    for j in range(per):
        plate = order[me_t * per + j]
        header = jnp.zeros((1, nx), jnp.float32)
        for at in range(blocks):
            for k in range(4):
                mine = lane1 + at * nx == plate + k * plates
                header = header + jnp.where(mine, contrib[at], 0.0)
        header = jnp.sum(header, axis=1, keepdims=True)
        row = jnp.where(lane1 == j, conduct[j] * (header * scale - level[j]), row)
    flow[...] = row[:, :per]

    for repeat in range(2):
        sums(repeat)[2]()
    halo_sent(ext, (pl.ds(0, 2),), h1s, h1r)
    halo_sent(ext, (2,), h2s, h2r)


def deliver(sol, res, flow, sol_out, res_out, flow_out, sems):
    copies = [
        pltpu.make_async_copy(src, dst, sems.at[at])
        for at, (src, dst) in enumerate([(sol, sol_out), (res, res_out), (flow, flow_out)])
    ]
    for copy in copies:
        copy.start()
    for copy in copies:
        copy.wait()


def on_device(n_slab, n_tile, right_side, diagonal, inlet_index, plate_order, conductance, plate_level):
    cz, cy, nx = right_side.shape
    inlet_index = inlet_index.transpose(0, 1, 3, 2)
    inlets, plates = inlet_index.shape[2:]
    per = conductance.shape[0]
    z_all, y_all = cz + 2 * HALO, cy + 2 * PAD
    count = n_slab * n_tile
    rows = 1 + 2 * -(-4 * plates // nx)
    rows2 = 8 * -(-rows // 8)
    f32, i32 = jnp.float32, jnp.int32
    block = jax.ShapeDtypeStruct((cz, cy, nx), f32)
    shapes = (block, block, jax.ShapeDtypeStruct((1, per), f32))
    dma = pltpu.SemaphoreType.DMA
    results = pl.pallas_call(
        functools.partial(kernel, n_slab, n_tile),
        out_shape=tuple(pltpu.VMEM(leaf.shape, leaf.dtype) for leaf in shapes),
        in_specs=[ANY] * 6,
        out_specs=(VMEM,) * 3,
        scratch_shapes=[
            pltpu.VMEM((3, z_all, y_all, nx), f32),
            pltpu.VMEM((4, z_all, y_all, nx), f32),
            pltpu.VMEM((z_all, y_all, nx), f32),
            pltpu.VMEM((z_all, y_all, nx), f32),
            pltpu.VMEM((inlets, plates), i32),
            pltpu.VMEM((inlets, plates, 2 * nx), jnp.bfloat16),
            pltpu.VMEM((inlets, plates, nx), f32),
            pltpu.VMEM((2, 8, nx), f32),
            pltpu.VMEM((rows, nx), f32),
            pltpu.SMEM(plate_order.shape, i32),
            pltpu.SMEM((per,), f32),
            pltpu.SMEM((per,), f32),
            pltpu.VMEM((2, rows2, nx), f32),
            pltpu.VMEM((2, count, rows2, nx), f32),
            dma((8,)), dma((8,)), dma((8,)), dma((8,)),
            dma((2,)), dma((2,)), dma((6,)),
        ],
        compiler_params=pltpu.CompilerParams(
            collective_id=0, has_side_effects=True, vmem_limit_bytes=60 * 1024 * 1024
        ),
    )(right_side, diagonal, inlet_index, plate_order, conductance, plate_level)
    sol, res, flow = pl.pallas_call(
        deliver,
        out_shape=shapes,
        in_specs=[VMEM] * 3,
        out_specs=(ANY,) * 3,
        scratch_shapes=[dma((3,))],
        compiler_params=pltpu.CompilerParams(vmem_limit_bytes=1024 * 1024),
    )(*results)
    return sol, res, flow.reshape(per)


def solution(mesh):
    in_specs = (
        P("slab", "tile", None),
        P("slab", "tile", None),
        P("slab", "tile", None, None),
        P(),
        P("tile"),
        P("tile"),
    )
    out_specs = (P("slab", "tile", None), P("slab", "tile", None), P("tile"))
    return jax.shard_map(
        functools.partial(on_device, mesh.shape["slab"], mesh.shape["tile"]),
        mesh=mesh, in_specs=in_specs, out_specs=out_specs, check_vma=False,
    )
```
